32 devices in a mesh: blk: 8 (over z, y), grp: 4 (over x, core).
Axes of the slice: x: 2, y: 2, z: 4, core: 2. Of those that a mesh axis runs over, the one named last changes fastest.
Arguments:
- users: float32 [8192, 256], P(('blk', 'grp')), may hold values from -1.5 to 1.5
- items: float32 [8192, 256], P('blk'), may hold values from -1.5 to 1.5
- noise_users: float32 [2, 8192, 256], P(None, ('blk', 'grp')), may hold values from -6 to 6
- noise_items: float32 [2, 8192, 256], P(None, 'blk'), may hold values from -6 to 6
- tile_index: int32 [2, 256], P(None, ('blk', 'grp')), may hold values from 0 to 15, as said below
- counts: int32 [2, 32], P(None, ('blk', 'grp')), may hold values from 1 to 8, as said below
- ratings: bfloat16 [2, 256, 128, 128], P(None, ('blk', 'grp')), may hold values from -6 to 6
- weights: bfloat16 [2, 256, 128, 128], P(None, ('blk', 'grp')), may hold values from 0 to 2
Outputs:
- users_out: float32 [8192, 256], P(('blk', 'grp'))
- items_out: float32 [8192, 256], P(('blk', 'grp'))
The draws below stay inside these ranges and needn't reach their ends.
Inputs may be any that keep to these rules, and one draw needn't show every extreme that they name: `tile_index`: slot t names user tile row t // 8 of the device's users and item tile column t % 8; the live slots of a device in a stratum name distinct tiles. `counts`: in every stratum some device has 8 live slots.
All inputs are finite; a program needn't handle non-finite values.
Results may differ from the reference program's by a relative error of at most 0.0003.
Values sent between devices are 32-bit elements; how exact they have to be, the bound alone decides.
A program may use at most 64 MiB of HBM per device.

```python
import math
import jax
import jax.numpy as jnp
from jax import lax

K = 256
TILE = 128
UB = 1024
IB = 1024
STRATA = 2
MAXT = 8
USERS = 8192
ITEMS = 8192
SLOTS = 256
N_BLK = 8
N_GRP = 4


def draw_tile_index(key, part):
    cells = UB // (N_GRP * TILE) * (IB // TILE)
    devices_all = N_BLK * N_GRP
    keys = jax.random.split(key, STRATA * devices_all)
    rows = jax.vmap(lambda single: jax.random.permutation(single, cells)[:MAXT])(keys)
    return rows.reshape(STRATA, devices_all * MAXT).astype(jnp.int32)


def draw_counts(key, part):
    devices_all = N_BLK * N_GRP
    floor_count = max(1, MAXT * 5 // 8)
    first = jax.random.randint(jax.random.fold_in(key, 11), (STRATA, devices_all), floor_count, MAXT + 1)
    second = jax.random.randint(jax.random.fold_in(key, 12), (STRATA, devices_all), floor_count, MAXT + 1)
    lower = jnp.minimum(first, second)
    chosen = jax.random.randint(jax.random.fold_in(key, 13), (STRATA, 1), 0, devices_all)
    filled = jnp.arange(devices_all)[None, :] == chosen
    return jnp.where(filled, MAXT, lower).astype(jnp.int32)


def draw_weights(key, part):
    shape = (STRATA, N_BLK * N_GRP * MAXT, TILE, TILE)
    keep = jax.random.uniform(jax.random.fold_in(key, 21), shape, jnp.float32) < 0.7
    level = 0.5 + jax.random.uniform(jax.random.fold_in(key, 22), shape, jnp.float32)
    return jnp.where(keep, level, 0.0).astype(jnp.bfloat16)


def steps_of(stream_key, extent, shards, least, largest):
    loudness = 1.0
    for dim, parts in shards:
        draws = jax.random.uniform(jax.random.fold_in(jax.random.fold_in(stream_key, 6), dim), (parts,), jnp.float32, least / len(shards), largest / len(shards))
        loudness = loudness * jnp.repeat(jnp.exp(draws), extent[dim] // parts).reshape((-1,) + (1,) * (len(extent) - 1 - dim))
    return loudness


def centred(rng, shape, scale, bound, shards=(), dtype=jnp.bfloat16):
    drawn = scale * jax.random.normal(rng, shape, jnp.float32)
    if shards:
        drawn = drawn * steps_of(rng, shape, shards, -0.22, 0.18)
    return jnp.clip(drawn, -bound, bound).astype(dtype)


def setup_inputs(seed: int = 0) -> dict:
    key_of = jax.random.split(jax.random.key(seed), 9)
    return {
        "users": centred(key_of[0], (USERS, K), 0.25, 1.5, ((0, 32),), jnp.float32),
        "items": centred(key_of[1], (ITEMS, K), 0.25, 1.5, ((0, 8),), jnp.float32),
        "noise_users": centred(key_of[2], (STRATA, USERS, K), 1.0, 6.0, ((1, 32),), jnp.float32),
        "noise_items": centred(key_of[3], (STRATA, ITEMS, K), 1.0, 6.0, ((1, 8),), jnp.float32),
        "tile_index": draw_tile_index(jax.random.fold_in(key_of[8], 71), 0),
        "counts": draw_counts(jax.random.fold_in(key_of[8], 71), 0),
        "ratings": centred(key_of[6], (STRATA, SLOTS, TILE, TILE), 1.0, 6.0, ((1, 32),)),
        "weights": draw_weights(jax.random.fold_in(key_of[8], 71), 0),
    }


STEP_SIZE = 0.001
LIKELIHOOD = 20.0
NOISE_SCALE = math.sqrt(0.002)
HIGHEST = lax.Precision.HIGHEST

def slot_terms(user_rows, item_block, slot_index, live_slots, rating_tiles, weight_tiles):
    tile = rating_tiles.shape[-1]
    rank = user_rows.shape[1]
    user_tiles = user_rows.shape[0] // tile
    item_tiles = item_block.shape[0] // tile
    tile_row = slot_index // item_tiles
    tile_col = slot_index % item_tiles
    user_table = user_rows.reshape(user_tiles, tile, rank)
    item_table = item_block.reshape(item_tiles, tile, rank)
    user_part = jnp.take(user_table, tile_row, axis=0)
    item_part = jnp.take(item_table, tile_col, axis=0)
    predicted = jnp.einsum('mik,mjk->mij', user_part, item_part, precision=HIGHEST)
    errors = live_slots[:, None, None] * weight_tiles.astype(jnp.float32) * (rating_tiles.astype(jnp.float32) - predicted)
    user_grads = jnp.einsum('mij,mjk->mik', errors, item_part, precision=HIGHEST)
    item_grads = jnp.einsum('mij,mik->mjk', errors, user_part, precision=HIGHEST)
    pick_user = (tile_row[:, None] == jnp.arange(user_tiles)[None, :]).astype(jnp.float32)
    pick_item = (tile_col[:, None] == jnp.arange(item_tiles)[None, :]).astype(jnp.float32)
    grad_users = jnp.einsum('mq,mik->qik', pick_user, user_grads, precision=HIGHEST).reshape(user_tiles * tile, rank)
    grad_items = jnp.einsum('mq,mjk->qjk', pick_item, item_grads, precision=HIGHEST).reshape(item_tiles * tile, rank)
    return (grad_users, grad_items)

def reference(users, items, noise_users, noise_items, tile_index, counts, ratings, weights):
    rank = users.shape[1]
    quarter = UB // N_GRP
    user_now = users
    position = items
    for stratum in range(STRATA):
        user_four = user_now.reshape(N_BLK, N_GRP, quarter, rank)
        blocks = position.reshape(N_BLK, IB, rank)
        slot_ids = tile_index[stratum].reshape(N_BLK, N_GRP, MAXT)
        live_counts = counts[stratum].reshape(N_BLK, N_GRP)
        rating_all = ratings[stratum].reshape(N_BLK, N_GRP, MAXT, TILE, TILE)
        weight_all = weights[stratum].reshape(N_BLK, N_GRP, MAXT, TILE, TILE)

        def one_block(inputs):
            user_block, item_block, block_ids, block_counts, block_ratings, block_weights = inputs

            def member(member_users, member_ids, member_count, member_ratings, member_weights):
                live_slots = (jnp.arange(MAXT) < member_count).astype(jnp.float32)
                return slot_terms(member_users, item_block, member_ids, live_slots, member_ratings, member_weights)
            grad_users, grad_items = jax.vmap(member)(user_block, block_ids, block_counts, block_ratings, block_weights)
            return (grad_users, lax.optimization_barrier(jnp.sum(grad_items, axis=0)))
        grad_users, grad_items = lax.map(one_block, (user_four, blocks, slot_ids, live_counts, rating_all, weight_all))
        grad_users = grad_users.reshape(USERS, rank)
        grad_items = grad_items.reshape(ITEMS, rank)
        user_now = user_now + STEP_SIZE * (LIKELIHOOD * grad_users - user_now) + NOISE_SCALE * noise_users[stratum]
        position = position + STEP_SIZE * (LIKELIHOOD * grad_items - position) + NOISE_SCALE * noise_items[stratum]
        position = jnp.roll(position, IB, axis=0)
    return (user_now, position)
```

```python
import functools
import math

import jax
import jax.numpy as jnp
from jax import lax
from jax.experimental import pallas as pl
from jax.experimental.pallas import tpu as pltpu
from jax.sharding import PartitionSpec as P

STEP_SIZE = 0.001
LIKELIHOOD = 20.0
NOISE_SCALE = math.sqrt(0.002)
TILE = 128
CHUNKS = 4
MESH = pl.DeviceIdType.MESH
F32 = jnp.float32
BF16 = jnp.bfloat16

(S0_SIB_FAR, S0_X, S0_SIB_OWN, FORWARD, RELAY_SIB, RELAY_X, RELAY_LAST,
 S1_SIB_FAR, S1_X, S1_SIB_OWN, FINAL) = range(11)
KINDS = 11


def halves(value):
    high = value.astype(BF16)
    low = (value - high.astype(F32)).astype(BF16)
    return high, low


def dot3(left, right, contract):
    dims = (contract, ((), ()))
    dot = functools.partial(lax.dot_general, dimension_numbers=dims, preferred_element_type=F32)
    return dot(left[0], right[0]) + (dot(left[0], right[1]) + dot(left[1], right[0]))


def kernel(n_blk, tiles, counts, users_hbm, items_hbm, noise_users_hbm, noise_items_hbm,
           ratings_hbm, weights_hbm, users_out, items_out,
           users, items, position, noise_users, noise_items, ratings0, ratings1, weights0, weights1,
           u_high, u_low, v_high, v_low, e_high, e_low, part, from_sib_far, from_x,
           from_sib_own, moved, users_new, local_sem, out_sem, send_sem, recv_sem):
    quarter = users.shape[0]
    chunk = quarter // CHUNKS
    item_tiles = items.shape[0] // TILE
    slots = tiles.shape[1]
    blk = lax.axis_index("blk")
    grp = lax.axis_index("grp")
    side = grp // 2
    core = grp % 2
    sibling = (blk, side * 2 + (1 - core))
    across = (blk, (1 - side) * 2 + core)
    ahead = ((blk + 1) % n_blk, grp)
    behind = ((blk + n_blk - 1) % n_blk, grp)
    q_a = (1 - side) * 2 + core
    q_b = (1 - side) * 2 + (1 - core)
    q_c = side * 2 + core
    q_d = side * 2 + (1 - core)

    def rows(q, k=None):
        if k is None:
            return pl.ds(pl.multiple_of(q * quarter, quarter), quarter)
        return pl.ds(pl.multiple_of(q * quarter + k * chunk, chunk), chunk)

    def piece(k):
        return pl.ds(k * chunk, chunk)

    loads = [
        pltpu.make_async_copy(users_hbm, users, local_sem.at[0]),
        pltpu.make_async_copy(items_hbm, items, local_sem.at[1]),
        pltpu.make_async_copy(ratings_hbm.at[0], ratings0, local_sem.at[2]),
        pltpu.make_async_copy(weights_hbm.at[0], weights0, local_sem.at[3]),
        pltpu.make_async_copy(noise_items_hbm.at[0, rows(q_a)], noise_items.at[0], local_sem.at[4]),
        pltpu.make_async_copy(noise_users_hbm, noise_users, local_sem.at[5]),
        pltpu.make_async_copy(ratings_hbm.at[1], ratings1, local_sem.at[6]),
        pltpu.make_async_copy(weights_hbm.at[1], weights1, local_sem.at[7]),
        pltpu.make_async_copy(noise_items_hbm.at[1, rows(q_c)], noise_items.at[1], local_sem.at[8]),
    ]
    for load in loads:
        load.start()

    barrier = pltpu.get_barrier_semaphore()
    for other in (sibling, across, ahead, behind):
        pl.semaphore_signal(barrier, inc=1, device_id=other, device_id_type=MESH)

    def remote(kind, k, source, target, device):
        return pltpu.make_async_remote_copy(
            src_ref=source, dst_ref=target, send_sem=send_sem.at[kind, k],
            recv_sem=recv_sem.at[kind, k], device_id=device, device_id_type=MESH)

    def copy_of(kind, k):
        if kind in (S0_SIB_FAR, S1_SIB_FAR):
            s = 0 if kind == S0_SIB_FAR else 1
            return remote(kind, k, part.at[s, 0, piece(k)], from_sib_far.at[s, piece(k)], sibling)
        if kind in (S0_X, S1_X):
            s = 0 if kind == S0_X else 1
            return remote(kind, k, part.at[s, 1, piece(k)], from_x.at[s, piece(k)], across)
        if kind in (S0_SIB_OWN, S1_SIB_OWN):
            s = 0 if kind == S0_SIB_OWN else 1
            return remote(kind, k, part.at[s, 2, piece(k)], from_sib_own.at[s, piece(k)], sibling)
        if kind == FORWARD:
            return remote(kind, k, moved.at[0, piece(k)], position.at[rows(q_a, k)], ahead)
        if kind == RELAY_SIB:
            return remote(kind, k, position.at[rows(q_a, k)], position.at[rows(q_a, k)], sibling)
        if kind == RELAY_X:
            return remote(kind, k, position.at[rows(q_a, k)], position.at[rows(q_a, k)], across)
        if kind == RELAY_LAST:
            return remote(kind, k, position.at[rows(q_c, k)], position.at[rows(q_c, k)], sibling)
        return remote(kind, k, moved.at[1, piece(k)], items_out.at[piece(k)], ahead)

    def send(kind, k):
        copy_of(kind, k).start()

    def arrive(kind, k):
        copy_of(kind, k).wait_recv()

    def cell(stratum, row, column):
        wanted = row * item_tiles + column
        slot = jnp.int32(0)
        live = jnp.float32(0)
        for s in range(slots):
            hit = jnp.logical_and(tiles[stratum, s] == wanted, s < counts[stratum, 0])
            slot = jnp.where(hit, s, slot)
            live = jnp.where(hit, jnp.float32(1), live)
        ratings, weights = ((ratings0, weights0), (ratings1, weights1))[stratum]
        return (ratings[slot].astype(F32), weights[slot].astype(F32) * live)

    def grads(stratum, place, q, block):
        user_parts = (u_high[...], u_low[...])
        v_high[place], v_low[place] = halves(block[rows(q), :])
        predicted = dot3(user_parts, (v_high[place], v_low[place]), ((1,), (1,)))
        bands = []
        for r in range(quarter // TILE):
            line = []
            for j in range(quarter // TILE):
                rating, weight = cell(stratum, r, q * (quarter // TILE) + j)
                line.append(weight * (rating - predicted[r * TILE:(r + 1) * TILE, j * TILE:(j + 1) * TILE]))
            bands.append(jnp.concatenate(line, axis=1))
        err = jnp.concatenate(bands, axis=0)
        e_high[place], e_low[place] = halves(err)
        return dot3(halves(err.T), user_parts, ((1,), (0,)))

    def user_step(stratum, now):
        total = jnp.zeros(now.shape, F32)
        for place in range(4):
            total += dot3((e_high[place], e_low[place]), (v_high[place], v_low[place]), ((1,), (0,)))
        return now + STEP_SIZE * (LIKELIHOOD * total - now) + NOISE_SCALE * noise_users[stratum]

    loads[0].wait()
    u_high[...], u_low[...] = halves(users[...])
    loads[1].wait()
    loads[2].wait()
    loads[3].wait()
    part[0, 0] = grads(0, 0, q_d, items)
    pl.semaphore_wait(barrier, 4)
    for k in range(CHUNKS):
        send(S0_SIB_FAR, k)
    part[0, 1] = grads(0, 1, q_c, items)
    for k in range(CHUNKS):
        arrive(S0_SIB_FAR, k)
        part[0, 1, piece(k)] += from_sib_far[0, piece(k)]
        send(S0_X, k)
    part[0, 2] = grads(0, 2, q_b, items)
    for k in range(CHUNKS):
        send(S0_SIB_OWN, k)
    part[0, 3] = grads(0, 3, q_a, items)
    loads[4].wait()
    for k in range(CHUNKS):
        arrive(S0_SIB_OWN, k)
        arrive(S0_X, k)
        now = items[rows(q_a, k), :]
        total = part[0, 3, piece(k)] + from_sib_own[0, piece(k)] + from_x[0, piece(k)]
        moved[0, piece(k)] = (now + STEP_SIZE * (LIKELIHOOD * total - now)
                              + NOISE_SCALE * noise_items[0, piece(k)])
        send(FORWARD, k)
    loads[5].wait()
    users_new[...] = user_step(0, users[...])
    u_high[...], u_low[...] = halves(users_new[...])

    for k in range(CHUNKS):
        arrive(FORWARD, k)
        send(RELAY_X, k)
        send(RELAY_SIB, k)
    loads[6].wait()
    loads[7].wait()
    for k in range(CHUNKS):
        arrive(RELAY_SIB, k)
    part[1, 0] = grads(1, 0, q_b, position)
    for k in range(CHUNKS):
        send(S1_SIB_FAR, k)
    part[1, 1] = grads(1, 1, q_a, position)
    for k in range(CHUNKS):
        arrive(S1_SIB_FAR, k)
        part[1, 1, piece(k)] += from_sib_far[1, piece(k)]
        send(S1_X, k)
    for k in range(CHUNKS):
        arrive(RELAY_X, k)
        send(RELAY_LAST, k)
    part[1, 3] = grads(1, 3, q_c, position)
    for k in range(CHUNKS):
        arrive(RELAY_LAST, k)
    part[1, 2] = grads(1, 2, q_d, position)
    for k in range(CHUNKS):
        send(S1_SIB_OWN, k)
    users_new[...] = user_step(1, users_new[...])
    store = pltpu.make_async_copy(users_new, users_out, out_sem)
    store.start()
    loads[8].wait()
    for k in range(CHUNKS):
        arrive(S1_SIB_OWN, k)
        arrive(S1_X, k)
        now = position[rows(q_c, k), :]
        total = part[1, 3, piece(k)] + from_sib_own[1, piece(k)] + from_x[1, piece(k)]
        moved[1, piece(k)] = (now + STEP_SIZE * (LIKELIHOOD * total - now)
                              + NOISE_SCALE * noise_items[1, piece(k)])
        send(FINAL, k)
    for kind in range(KINDS):
        for k in range(CHUNKS):
            copy_of(kind, k).wait_send()
    store.wait()
    for k in range(CHUNKS):
        arrive(FINAL, k)


def body(n_blk, users, items, noise_users, noise_items, tile_index, counts, ratings, weights):
    mine, rank = users.shape
    slots, tile = ratings.shape[1], ratings.shape[2]
    square = (mine, mine)
    kept = (mine, rank)
    any_spec = pl.BlockSpec(memory_space=pl.ANY)
    smem_spec = pl.BlockSpec(memory_space=pltpu.SMEM)
    work = 2 * 3 * 3 * 2 * mine * items.shape[0] * rank
    return pl.pallas_call(
        functools.partial(kernel, n_blk),
        out_shape=(jax.ShapeDtypeStruct(kept, F32), jax.ShapeDtypeStruct(kept, F32)),
        in_specs=[smem_spec, smem_spec] + [any_spec] * 6,
        out_specs=(any_spec, any_spec),
        scratch_shapes=[
            pltpu.VMEM(kept, F32),
            pltpu.VMEM(items.shape, F32),
            pltpu.VMEM(items.shape, F32),
            pltpu.VMEM((2,) + kept, F32),
            pltpu.VMEM((2,) + kept, F32),
            pltpu.VMEM((slots, tile, tile), BF16),
            pltpu.VMEM((slots, tile, tile), BF16),
            pltpu.VMEM((slots, tile, tile), BF16),
            pltpu.VMEM((slots, tile, tile), BF16),
            pltpu.VMEM(kept, BF16),
            pltpu.VMEM(kept, BF16),
            pltpu.VMEM((4,) + kept, BF16),
            pltpu.VMEM((4,) + kept, BF16),
            pltpu.VMEM((4,) + square, BF16),
            pltpu.VMEM((4,) + square, BF16),
            pltpu.VMEM((2, 4) + kept, F32),
            pltpu.VMEM((2,) + kept, F32),
            pltpu.VMEM((2,) + kept, F32),
            pltpu.VMEM((2,) + kept, F32),
            pltpu.VMEM((2,) + kept, F32),
            pltpu.VMEM(kept, F32),
            pltpu.SemaphoreType.DMA((9,)),
            pltpu.SemaphoreType.DMA,
            pltpu.SemaphoreType.DMA((KINDS, CHUNKS)),
            pltpu.SemaphoreType.DMA((KINDS, CHUNKS)),
        ],
        compiler_params=pltpu.CompilerParams(
            collective_id=0, has_side_effects=True, vmem_limit_bytes=56 * 1024 * 1024),
        cost_estimate=pl.CostEstimate(flops=work, bytes_accessed=4 * 2 ** 20, transcendentals=0),
    )(tile_index, counts, users, items, noise_users, noise_items, ratings, weights)


def solution(mesh):
    in_specs = (
        P(("blk", "grp"), None),
        P("blk", None),
        P(None, ("blk", "grp"), None),
        P(None, "blk", None),
        P(None, ("blk", "grp")),
        P(None, ("blk", "grp")),
        P(None, ("blk", "grp"), None, None),
        P(None, ("blk", "grp"), None, None),
    )
    out_specs = (P(("blk", "grp"), None), P(("blk", "grp"), None))
    return jax.shard_map(functools.partial(body, mesh.shape["blk"]), mesh=mesh,
                         in_specs=in_specs, out_specs=out_specs, check_vma=False)
```

```python
import functools
import math

import jax
import jax.numpy as jnp
from jax import lax
from jax.experimental import pallas as pl
from jax.experimental.pallas import tpu as pltpu
from jax.sharding import PartitionSpec as P

STEP_SIZE = 0.001
LIKELIHOOD = 20.0
NOISE_SCALE = math.sqrt(0.002)
TILE = 128
CHUNKS = 4
LAG = 2
MESH = pl.DeviceIdType.MESH
F32 = jnp.float32
BF16 = jnp.bfloat16

(S0_SIB_FAR, S0_X, S0_SIB_OWN, FORWARD, RELAY_SIB, RELAY_X, RELAY_LAST,
 S1_SIB_FAR, S1_X, S1_SIB_OWN, FINAL) = range(11)
KINDS = 11


def halves(value):
    high = value.astype(BF16)
    low = (value - high.astype(F32)).astype(BF16)
    return high, low


def dot3(left, right, contract):
    dims = (contract, ((), ()))
    dot = functools.partial(lax.dot_general, dimension_numbers=dims, preferred_element_type=F32)
    return dot(left[0], right[0]) + (dot(left[0], right[1]) + dot(left[1], right[0]))


def kernel(n_blk, tiles, counts, users_hbm, items_hbm, noise_users_hbm, noise_items_hbm,
           ratings_hbm, weights_hbm, users_out, items_out,
           users, items, position, noise_users, noise_items, ratings0, ratings1, weights0, weights1,
           u_high, u_low, v_high, v_low, e_high, e_low, part, from_sib_far, from_x,
           from_sib_own, moved, users_new, local_sem, out_sem, send_sem, recv_sem):
    quarter = users.shape[0]
    chunk = quarter // CHUNKS
    item_tiles = items.shape[0] // TILE
    slots = tiles.shape[1]
    blk = lax.axis_index("blk")
    grp = lax.axis_index("grp")
    side = grp // 2
    core = grp % 2
    sibling = (blk, side * 2 + (1 - core))
    across = (blk, (1 - side) * 2 + core)
    ahead = ((blk + 1) % n_blk, grp)
    behind = ((blk + n_blk - 1) % n_blk, grp)
    q_a = (1 - side) * 2 + core
    q_b = (1 - side) * 2 + (1 - core)
    q_c = side * 2 + core
    q_d = side * 2 + (1 - core)

    def rows(q, k=None):
        if k is None:
            return pl.ds(pl.multiple_of(q * quarter, quarter), quarter)
        return pl.ds(pl.multiple_of(q * quarter + k * chunk, chunk), chunk)

    def piece(k):
        return pl.ds(k * chunk, chunk)

    loads = [
        pltpu.make_async_copy(users_hbm, users, local_sem.at[0]),
        pltpu.make_async_copy(items_hbm, items, local_sem.at[1]),
        pltpu.make_async_copy(ratings_hbm.at[0], ratings0, local_sem.at[2]),
        pltpu.make_async_copy(weights_hbm.at[0], weights0, local_sem.at[3]),
        pltpu.make_async_copy(noise_items_hbm.at[0, rows(q_a)], noise_items.at[0], local_sem.at[4]),
        pltpu.make_async_copy(noise_users_hbm, noise_users, local_sem.at[5]),
        pltpu.make_async_copy(ratings_hbm.at[1], ratings1, local_sem.at[6]),
        pltpu.make_async_copy(weights_hbm.at[1], weights1, local_sem.at[7]),
        pltpu.make_async_copy(noise_items_hbm.at[1, rows(q_c)], noise_items.at[1], local_sem.at[8]),
    ]
    for load in loads:
        load.start()

    barrier = pltpu.get_barrier_semaphore()
    for other in (sibling, across, ahead, behind):
        pl.semaphore_signal(barrier, inc=1, device_id=other, device_id_type=MESH)

    def remote(kind, k, source, target, device):
        return pltpu.make_async_remote_copy(
            src_ref=source, dst_ref=target, send_sem=send_sem.at[kind, k],
            recv_sem=recv_sem.at[kind, k], device_id=device, device_id_type=MESH)

    def copy_of(kind, k):
        if kind in (S0_SIB_FAR, S1_SIB_FAR):
            s = 0 if kind == S0_SIB_FAR else 1
            return remote(kind, k, part.at[s, 0, piece(k)], from_sib_far.at[s, piece(k)], sibling)
        if kind in (S0_X, S1_X):
            s = 0 if kind == S0_X else 1
            return remote(kind, k, part.at[s, 1, piece(k)], from_x.at[s, piece(k)], across)
        if kind in (S0_SIB_OWN, S1_SIB_OWN):
            s = 0 if kind == S0_SIB_OWN else 1
            return remote(kind, k, part.at[s, 2, piece(k)], from_sib_own.at[s, piece(k)], sibling)
        if kind == FORWARD:
            return remote(kind, k, moved.at[0, piece(k)], position.at[rows(q_a, k)], ahead)
        if kind == RELAY_SIB:
            return remote(kind, k, position.at[rows(q_a, k)], position.at[rows(q_a, k)], sibling)
        if kind == RELAY_X:
            return remote(kind, k, position.at[rows(q_a, k)], position.at[rows(q_a, k)], across)
        if kind == RELAY_LAST:
            return remote(kind, k, position.at[rows(q_c, k)], position.at[rows(q_c, k)], sibling)
        return remote(kind, k, moved.at[1, piece(k)], items_out.at[piece(k)], ahead)

    def send(kind, k):
        copy_of(kind, k).start()

    def arrive(kind, k):
        copy_of(kind, k).wait_recv()

    def cell(stratum, row, column):
        wanted = row * item_tiles + column
        slot = jnp.int32(0)
        live = jnp.float32(0)
        for s in range(slots):
            hit = jnp.logical_and(tiles[stratum, s] == wanted, s < counts[0, stratum])
            slot = jnp.where(hit, s, slot)
            live = jnp.where(hit, jnp.float32(1), live)
        ratings, weights = ((ratings0, weights0), (ratings1, weights1))[stratum]
        return (ratings[slot].astype(F32), weights[slot].astype(F32) * live)

    def grads(stratum, place, q, block):
        user_parts = (u_high[...], u_low[...])
        v_high[place], v_low[place] = halves(block[rows(q), :])
        predicted = dot3(user_parts, (v_high[place], v_low[place]), ((1,), (1,)))
        bands = []
        for r in range(quarter // TILE):
            line = []
            for j in range(quarter // TILE):
                rating, weight = cell(stratum, r, q * (quarter // TILE) + j)
                line.append(weight * (rating - predicted[r * TILE:(r + 1) * TILE, j * TILE:(j + 1) * TILE]))
            bands.append(jnp.concatenate(line, axis=1))
        err = jnp.concatenate(bands, axis=0)
        e_high[place], e_low[place] = halves(err)
        return dot3(halves(err.T), user_parts, ((1,), (0,)))

    def user_step(stratum, now):
        total = jnp.zeros(now.shape, F32)
        for place in range(4):
            total += dot3((e_high[place], e_low[place]), (v_high[place], v_low[place]), ((1,), (0,)))
        return now + STEP_SIZE * (LIKELIHOOD * total - now) + NOISE_SCALE * noise_users[stratum]

    loads[0].wait()
    u_high[...], u_low[...] = halves(users[...])
    loads[1].wait()
    loads[2].wait()
    loads[3].wait()
    part[0, 0] = grads(0, 0, q_d, items)
    pl.semaphore_wait(barrier, 4)
    for k in range(CHUNKS):
        send(S0_SIB_FAR, k)
    part[0, 1] = grads(0, 1, q_c, items)
    for k in range(CHUNKS):
        arrive(S0_SIB_FAR, k)
        part[0, 1, piece(k)] += from_sib_far[0, piece(k)]
        send(S0_X, k)
    part[0, 2] = grads(0, 2, q_b, items)
    for k in range(CHUNKS):
        send(S0_SIB_OWN, k)
    part[0, 3] = grads(0, 3, q_a, items)
    loads[4].wait()
    loads[5].wait()
    users_new[...] = user_step(0, users[...])
    u_high[...], u_low[...] = halves(users_new[...])

    for k in range(CHUNKS + LAG):
        if k < CHUNKS:
            arrive(S0_SIB_OWN, k)
            arrive(S0_X, k)
            now = items[rows(q_a, k), :]
            total = part[0, 3, piece(k)] + from_sib_own[0, piece(k)] + from_x[0, piece(k)]
            moved[0, piece(k)] = (now + STEP_SIZE * (LIKELIHOOD * total - now)
                                  + NOISE_SCALE * noise_items[0, piece(k)])
            send(FORWARD, k)
        if k >= LAG:
            arrive(FORWARD, k - LAG)
            send(RELAY_X, k - LAG)
            send(RELAY_SIB, k - LAG)
    loads[6].wait()
    loads[7].wait()
    for k in range(CHUNKS):
        arrive(RELAY_SIB, k)
    part[1, 0] = grads(1, 0, q_b, position)
    for k in range(CHUNKS):
        send(S1_SIB_FAR, k)
    part[1, 1] = grads(1, 1, q_a, position)
    for k in range(CHUNKS):
        arrive(S1_SIB_FAR, k)
        part[1, 1, piece(k)] += from_sib_far[1, piece(k)]
        send(S1_X, k)
    for k in range(CHUNKS):
        arrive(RELAY_X, k)
        send(RELAY_LAST, k)
    part[1, 3] = grads(1, 3, q_c, position)
    for k in range(CHUNKS):
        arrive(RELAY_LAST, k)
    part[1, 2] = grads(1, 2, q_d, position)
    for k in range(CHUNKS):
        send(S1_SIB_OWN, k)
    users_new[...] = user_step(1, users_new[...])
    store = pltpu.make_async_copy(users_new, users_out, out_sem)
    store.start()
    loads[8].wait()
    for k in range(CHUNKS):
        arrive(S1_SIB_OWN, k)
        arrive(S1_X, k)
        now = position[rows(q_c, k), :]
        total = part[1, 3, piece(k)] + from_sib_own[1, piece(k)] + from_x[1, piece(k)]
        moved[1, piece(k)] = (now + STEP_SIZE * (LIKELIHOOD * total - now)
                              + NOISE_SCALE * noise_items[1, piece(k)])
        send(FINAL, k)
    for kind in range(KINDS):
        for k in range(CHUNKS):
            copy_of(kind, k).wait_send()
    store.wait()
    for k in range(CHUNKS):
        arrive(FINAL, k)


def body(n_blk, users, items, noise_users, noise_items, tile_index, counts, ratings, weights):
    mine, rank = users.shape
    slots, tile = ratings.shape[1], ratings.shape[2]
    square = (mine, mine)
    kept = (mine, rank)
    any_spec = pl.BlockSpec(memory_space=pl.ANY)
    smem_spec = pl.BlockSpec(memory_space=pltpu.SMEM)
    work = 2 * 3 * 3 * 2 * mine * items.shape[0] * rank
    return pl.pallas_call(
        functools.partial(kernel, n_blk),
        out_shape=(pltpu.VMEM(kept, F32), pltpu.VMEM(kept, F32)),
        in_specs=[smem_spec, smem_spec] + [any_spec] * 6,
        out_specs=(any_spec, any_spec),
        scratch_shapes=[
            pltpu.VMEM(kept, F32),
            pltpu.VMEM(items.shape, F32),
            pltpu.VMEM(items.shape, F32),
            pltpu.VMEM((2,) + kept, F32),
            pltpu.VMEM((2,) + kept, F32),
            pltpu.VMEM((slots, tile, tile), BF16),
            pltpu.VMEM((slots, tile, tile), BF16),
            pltpu.VMEM((slots, tile, tile), BF16),
            pltpu.VMEM((slots, tile, tile), BF16),
            pltpu.VMEM(kept, BF16),
            pltpu.VMEM(kept, BF16),
            pltpu.VMEM((4,) + kept, BF16),
            pltpu.VMEM((4,) + kept, BF16),
            pltpu.VMEM((4,) + square, BF16),
            pltpu.VMEM((4,) + square, BF16),
            pltpu.VMEM((2, 4) + kept, F32),
            pltpu.VMEM((2,) + kept, F32),
            pltpu.VMEM((2,) + kept, F32),
            pltpu.VMEM((2,) + kept, F32),
            pltpu.VMEM((2,) + kept, F32),
            pltpu.VMEM(kept, F32),
            pltpu.SemaphoreType.DMA((9,)),
            pltpu.SemaphoreType.DMA,
            pltpu.SemaphoreType.DMA((KINDS, CHUNKS)),
            pltpu.SemaphoreType.DMA((KINDS, CHUNKS)),
        ],
        compiler_params=pltpu.CompilerParams(
            collective_id=0, has_side_effects=True, vmem_limit_bytes=56 * 1024 * 1024),
        cost_estimate=pl.CostEstimate(flops=work, bytes_accessed=4 * 2 ** 20, transcendentals=0),
    )(tile_index, counts.T, users, items, noise_users, noise_items, ratings, weights)


def solution(mesh):
    in_specs = (
        P(("blk", "grp"), None),
        P("blk", None),
        P(None, ("blk", "grp"), None),
        P(None, "blk", None),
        P(None, ("blk", "grp")),
        P(None, ("blk", "grp")),
        P(None, ("blk", "grp"), None, None),
        P(None, ("blk", "grp"), None, None),
    )
    out_specs = (P(("blk", "grp"), None), P(("blk", "grp"), None))
    return jax.shard_map(functools.partial(body, mesh.shape["blk"]), mesh=mesh,
                         in_specs=in_specs, out_specs=out_specs, check_vma=False)
```

```python
import functools
import math

import jax
import jax.numpy as jnp
from jax import lax
from jax.experimental import pallas as pl
from jax.experimental.pallas import tpu as pltpu
from jax.sharding import PartitionSpec as P

STEP_SIZE = 0.001
LIKELIHOOD = 20.0
NOISE_SCALE = math.sqrt(0.002)
TILE = 128
FINE = 4
MESH = pl.DeviceIdType.MESH
F32 = jnp.float32
BF16 = jnp.bfloat16

(S0_SIB_FAR, S0_X, S0_SIB_OWN, FORWARD, RELAY_SIB, RELAY_X, RELAY_LAST,
 S1_SIB_FAR, S1_X, S1_SIB_OWN, FINAL) = range(11)
KINDS = 11
ON_CHIP = (S0_SIB_FAR, S0_SIB_OWN, RELAY_SIB, RELAY_LAST, S1_SIB_FAR, S1_SIB_OWN)


def halves(value):
    high = value.astype(BF16)
    low = (value - high.astype(F32)).astype(BF16)
    return high, low


def dot3(left, right, contract):
    dims = (contract, ((), ()))
    dot = functools.partial(lax.dot_general, dimension_numbers=dims, preferred_element_type=F32)
    return dot(left[0], right[0]) + (dot(left[0], right[1]) + dot(left[1], right[0]))


def kernel(n_blk, tiles_hbm, counts_hbm, users_hbm, items_hbm, noise_users_hbm, noise_items_hbm,
           ratings_hbm, weights_hbm, users_out, items_out,
           tiles, counts, users, items, position, noise_users, noise_items, ratings0, ratings1, weights0, weights1,
           u_high, u_low, v_high, v_low, e_high, e_low, part, from_sib_far, from_x,
           from_sib_own, moved, users_new, local_sem, out_sem, send_sem, recv_sem):
    quarter = users.shape[0]
    per = quarter // TILE
    item_tiles = items.shape[0] // TILE
    slots = tiles.shape[1]
    blk = lax.axis_index("blk")
    grp = lax.axis_index("grp")
    side = grp // 2
    core = grp % 2
    sibling = (blk, side * 2 + (1 - core))
    across = (blk, (1 - side) * 2 + core)
    ahead = ((blk + 1) % n_blk, grp)
    behind = ((blk + n_blk - 1) % n_blk, grp)
    q_a = (1 - side) * 2 + core
    q_b = (1 - side) * 2 + (1 - core)
    q_c = side * 2 + core
    q_d = side * 2 + (1 - core)

    def rows(q, start=0, size=quarter):
        return pl.ds(pl.multiple_of(q * quarter + start, size), size)

    def chunk(kind):
        return TILE if kind in ON_CHIP else quarter // FINE

    def count(kind):
        return quarter // chunk(kind)

    def load(index, source, target):
        copy = pltpu.make_async_copy(source, target, local_sem.at[index])
        copy.start()
        return copy

    load_tiles = load(0, tiles_hbm, tiles)
    load_counts = load(1, counts_hbm, counts)
    load_users = load(2, users_hbm, users)
    load_items = [load(3, items_hbm.at[rows(q_d)], items.at[rows(q_d)])]
    load_ratings = [load(4, ratings_hbm.at[0], ratings0)]
    load_weights = [load(5, weights_hbm.at[0], weights0)]
    barrier = pltpu.get_barrier_semaphore()
    for other in (sibling, across, ahead, behind):
        pl.semaphore_signal(barrier, inc=1, device_id=other, device_id_type=MESH)
    for index, q in ((6, q_c), (7, q_b), (8, q_a)):
        load_items.append(load(index, items_hbm.at[rows(q)], items.at[rows(q)]))
    load_noise_users = load(9, noise_users_hbm, noise_users)
    load_noise_items = [load(10, noise_items_hbm.at[0, rows(q_a)], noise_items.at[0]),
                        load(11, noise_items_hbm.at[1, rows(q_c)], noise_items.at[1])]
    load_ratings.append(load(12, ratings_hbm.at[1], ratings1))
    load_weights.append(load(13, weights_hbm.at[1], weights1))

    def remote(kind, k, source, target, device):
        return pltpu.make_async_remote_copy(
            src_ref=source, dst_ref=target, send_sem=send_sem.at[kind, k],
            recv_sem=recv_sem.at[kind, k], device_id=device, device_id_type=MESH)

    def copy_of(kind, k):
        size = chunk(kind)
        piece = pl.ds(k * size, size)
        s = 0 if kind < S1_SIB_FAR else 1
        if kind in (S0_SIB_FAR, S1_SIB_FAR):
            return remote(kind, k, part.at[s, 0, piece], from_sib_far.at[s, piece], sibling)
        if kind in (S0_X, S1_X):
            return remote(kind, k, part.at[s, 1, piece], from_x.at[s, piece], across)
        if kind in (S0_SIB_OWN, S1_SIB_OWN):
            return remote(kind, k, part.at[s, 2, piece], from_sib_own.at[s, piece], sibling)
        if kind == FORWARD:
            return remote(kind, k, moved.at[0, piece], position.at[rows(q_a, k * size, size)], ahead)
        if kind == FINAL:
            return remote(kind, k, moved.at[1, piece], items_out.at[piece], ahead)
        where = rows(q_c if kind == RELAY_LAST else q_a, k * size, size)
        other = across if kind == RELAY_X else sibling
        return remote(kind, k, position.at[where], position.at[where], other)

    def send(kind, k):
        copy_of(kind, k).start()

    def arrive(kind, k):
        copy_of(kind, k).wait_recv()

    def cell(stratum, row, column):
        wanted = row * item_tiles + column
        slot = jnp.int32(0)
        live = jnp.float32(0)
        for s in range(slots):
            hit = jnp.logical_and(tiles[stratum, s] == wanted, s < counts[0, stratum])
            slot = jnp.where(hit, s, slot)
            live = jnp.where(hit, jnp.float32(1), live)
        ratings, weights = ((ratings0, weights0), (ratings1, weights1))[stratum]
        return (ratings[slot].astype(F32), weights[slot].astype(F32) * live)

    def grads(stratum, place, q, block, j):
        span = slice(j * TILE, (j + 1) * TILE)
        user_parts = (u_high[...], u_low[...])
        item_parts = halves(block[rows(q, j * TILE, TILE), :])
        v_high[place, span], v_low[place, span] = item_parts
        predicted = dot3(user_parts, item_parts, ((1,), (1,)))
        bands = []
        for r in range(per):
            rating, weight = cell(stratum, r, q * per + j)
            bands.append(weight * (rating - predicted[r * TILE:(r + 1) * TILE]))
        err = jnp.concatenate(bands, axis=0)
        e_high[place, :, span], e_low[place, :, span] = halves(err)
        part[stratum, place, span] = dot3(halves(err.T), user_parts, ((1,), (0,)))

    def send_far(stratum, j):
        span = slice(j * TILE, (j + 1) * TILE)
        arrive((S0_SIB_FAR, S1_SIB_FAR)[stratum], j)
        part[stratum, 1, span] += from_sib_far[stratum, span]
        kind = (S0_X, S1_X)[stratum]
        for k in range(j * FINE // per, (j + 1) * FINE // per):
            send(kind, k)

    def user_step(stratum, now):
        total = jnp.zeros(now.shape, F32)
        for place in range(4):
            total += dot3((e_high[place], e_low[place]), (v_high[place], v_low[place]), ((1,), (0,)))
        return now + STEP_SIZE * (LIKELIHOOD * total - now) + NOISE_SCALE * noise_users[stratum]

    def item_step(stratum, now, k):
        piece = pl.ds(k * quarter // FINE, quarter // FINE)
        arrive((S0_X, S1_X)[stratum], k)
        total = part[stratum, 3, piece] + from_sib_own[stratum, piece] + from_x[stratum, piece]
        moved[stratum, piece] = (now + STEP_SIZE * (LIKELIHOOD * total - now)
                                 + NOISE_SCALE * noise_items[stratum, piece])
        send((FORWARD, FINAL)[stratum], k)

    load_users.wait()
    u_high[...], u_low[...] = halves(users[...])
    load_tiles.wait()
    load_counts.wait()
    load_items[0].wait()
    load_ratings[0].wait()
    load_weights[0].wait()
    for j in range(per):
        grads(0, 0, q_d, items, j)
        if j == 0:
            pl.semaphore_wait(barrier, 4)
        send(S0_SIB_FAR, j)
    load_items[1].wait()
    for j in range(per):
        grads(0, 1, q_c, items, j)
        send_far(0, j)
    load_items[2].wait()
    for j in range(per):
        grads(0, 2, q_b, items, j)
        send(S0_SIB_OWN, j)
    load_items[3].wait()
    for j in range(per):
        grads(0, 3, q_a, items, j)
    load_noise_users.wait()
    users_new[...] = user_step(0, users[...])
    u_high[...], u_low[...] = halves(users_new[...])
    load_noise_items[0].wait()
    for load_late in (load_ratings[1], load_weights[1], load_noise_items[1]):
        load_late.wait()

    def relay(k):
        arrive(FORWARD, k)
        send(RELAY_X, k)
        if (k + 1) * per % FINE == 0:
            send(RELAY_SIB, (k + 1) * per // FINE - 1)

    fine = quarter // FINE
    for k in range(FINE):
        if k * per % FINE == 0:
            arrive(S0_SIB_OWN, k * per // FINE)
        item_step(0, items[rows(q_a, k * fine, fine), :], k)
        if k >= FINE - 2:
            relay(k - (FINE - 2))
    for j in range(per):
        arrive(RELAY_SIB, j)
        grads(1, 0, q_b, position, j)
        send(S1_SIB_FAR, j)
        if j == 0:
            relay(FINE - 2)
        grads(1, 1, q_a, position, j)
        send_far(1, j)
        if j == 0:
            relay(FINE - 1)
    for j in range(per):
        for k in range(j * FINE // per, (j + 1) * FINE // per):
            arrive(RELAY_X, k)
        send(RELAY_LAST, j)
        grads(1, 3, q_c, position, j)
    for j in range(per):
        arrive(RELAY_LAST, j)
        grads(1, 2, q_d, position, j)
        send(S1_SIB_OWN, j)
    users_new[...] = user_step(1, users_new[...])
    store = pltpu.make_async_copy(users_new, users_out, out_sem)
    store.start()
    for k in range(FINE):
        if k * per % FINE == 0:
            arrive(S1_SIB_OWN, k * per // FINE)
        item_step(1, position[rows(q_c, k * fine, fine), :], k)
    for kind in range(KINDS):
        for k in range(count(kind)):
            copy_of(kind, k).wait_send()
    store.wait()
    for k in range(FINE):
        arrive(FINAL, k)


def body(n_blk, users, items, noise_users, noise_items, tile_index, counts, ratings, weights):
    mine, rank = users.shape
    slots, tile = ratings.shape[1], ratings.shape[2]
    square = (mine, mine)
    kept = (mine, rank)
    any_spec = pl.BlockSpec(memory_space=pl.ANY)
    work = 2 * 3 * 3 * 2 * mine * items.shape[0] * rank
    return pl.pallas_call(
        functools.partial(kernel, n_blk),
        out_shape=(pltpu.VMEM(kept, F32), pltpu.VMEM(kept, F32)),
        in_specs=[any_spec] * 8,
        out_specs=(any_spec, any_spec),
        scratch_shapes=[
            pltpu.SMEM(tile_index.shape, jnp.int32),
            pltpu.SMEM((1, counts.shape[0]), jnp.int32),
            pltpu.VMEM(kept, F32),
            pltpu.VMEM(items.shape, F32),
            pltpu.VMEM(items.shape, F32),
            pltpu.VMEM((2,) + kept, F32),
            pltpu.VMEM((2,) + kept, F32),
            pltpu.VMEM((slots, tile, tile), BF16),
            pltpu.VMEM((slots, tile, tile), BF16),
            pltpu.VMEM((slots, tile, tile), BF16),
            pltpu.VMEM((slots, tile, tile), BF16),
            pltpu.VMEM(kept, BF16),
            pltpu.VMEM(kept, BF16),
            pltpu.VMEM((4,) + kept, BF16),
            pltpu.VMEM((4,) + kept, BF16),
            pltpu.VMEM((4,) + square, BF16),
            pltpu.VMEM((4,) + square, BF16),
            pltpu.VMEM((2, 4) + kept, F32),
            pltpu.VMEM((2,) + kept, F32),
            pltpu.VMEM((2,) + kept, F32),
            pltpu.VMEM((2,) + kept, F32),
            pltpu.VMEM((2,) + kept, F32),
            pltpu.VMEM(kept, F32),
            pltpu.SemaphoreType.DMA((14,)),
            pltpu.SemaphoreType.DMA,
            pltpu.SemaphoreType.DMA((KINDS, FINE)),
            pltpu.SemaphoreType.DMA((KINDS, FINE)),
        ],
        compiler_params=pltpu.CompilerParams(
            collective_id=0, has_side_effects=True, vmem_limit_bytes=56 * 1024 * 1024),
        cost_estimate=pl.CostEstimate(flops=work, bytes_accessed=4 * 2 ** 20, transcendentals=0),
    )(tile_index, counts.T, users, items, noise_users, noise_items, ratings, weights)


def solution(mesh):
    in_specs = (
        P(("blk", "grp"), None),
        P("blk", None),
        P(None, ("blk", "grp"), None),
        P(None, "blk", None),
        P(None, ("blk", "grp")),
        P(None, ("blk", "grp")),
        P(None, ("blk", "grp"), None, None),
        P(None, ("blk", "grp"), None, None),
    )
    out_specs = (P(("blk", "grp"), None), P(("blk", "grp"), None))
    return jax.shard_map(functools.partial(body, mesh.shape["blk"]), mesh=mesh,
                         in_specs=in_specs, out_specs=out_specs, check_vma=False)
```

```python
import functools
import math

import jax
import jax.numpy as jnp
from jax import lax
from jax.experimental import pallas as pl
from jax.experimental.pallas import tpu as pltpu
from jax.sharding import PartitionSpec as P

STEP_SIZE = 0.001
LIKELIHOOD = 20.0
NOISE_SCALE = math.sqrt(0.002)
TILE = 128
FINE = 4
MESH = pl.DeviceIdType.MESH
F32 = jnp.float32
BF16 = jnp.bfloat16

(S0_SIB_FAR, S0_X, S0_SIB_OWN, FORWARD, RELAY_SIB, RELAY_X, RELAY_LAST,
 S1_SIB_FAR, S1_X, S1_SIB_OWN, FINAL) = range(11)
KINDS = 11
ON_CHIP = (S0_SIB_FAR, S0_SIB_OWN, RELAY_SIB, RELAY_LAST, S1_SIB_FAR, S1_SIB_OWN)


def halves(value):
    high = value.astype(BF16)
    low = (value - high.astype(F32)).astype(BF16)
    return high, low


def dot(left, right, contract):
    return lax.dot_general(left, right, (contract, ((), ())), preferred_element_type=F32)


def left_triple(value, axis):
    high, low = halves(value)
    return jnp.concatenate([high, low, high], axis=axis)


def right_triple(value, axis):
    high, low = halves(value)
    return jnp.concatenate([high, high, low], axis=axis)


def kernel(n_blk, tiles_hbm, counts_hbm, users_hbm, items_hbm, noise_users_hbm, noise_items_hbm,
           ratings_hbm, weights_hbm, users_out, items_out,
           tiles, counts, users, blocks, noise_users, noise_items, ratings, weights,
           u_wide, u_tall, v_tall, e_wide, part, from_sib_far, from_x,
           from_sib_own, moved, local_sem, out_sem, send_sem, recv_sem):
    quarter = users.shape[0]
    per = quarter // TILE
    items = blocks.at[0]
    position = blocks.at[1]
    item_tiles = items.shape[0] // TILE
    slots = tiles.shape[1]
    blk = lax.axis_index("blk")
    grp = lax.axis_index("grp")
    side = grp // 2
    core = grp % 2
    sibling = (blk, side * 2 + (1 - core))
    across = (blk, (1 - side) * 2 + core)
    ahead = ((blk + 1) % n_blk, grp)
    behind = ((blk + n_blk - 1) % n_blk, grp)
    q_a = (1 - side) * 2 + core
    q_b = (1 - side) * 2 + (1 - core)
    q_c = side * 2 + core
    q_d = side * 2 + (1 - core)

    def rows(q, start=0, size=quarter):
        return pl.ds(pl.multiple_of(q * quarter + start, size), size)

    def chunk(kind):
        return TILE if kind in ON_CHIP else quarter // FINE

    def count(kind):
        return quarter // chunk(kind)

    def load(index, source, target):
        copy = pltpu.make_async_copy(source, target, local_sem.at[index])
        copy.start()
        return copy

    load_tiles = load(0, tiles_hbm, tiles)
    load_counts = load(1, counts_hbm, counts)
    load_users = load(2, users_hbm, users)
    load_items = [load(3, items_hbm.at[rows(q_d)], items.at[rows(q_d)])]
    load_ratings = load(4, ratings_hbm, ratings)
    load_weights = load(5, weights_hbm, weights)
    barrier = pltpu.get_barrier_semaphore()
    for other in (sibling, across, ahead, behind):
        pl.semaphore_signal(barrier, inc=1, device_id=other, device_id_type=MESH)
    for index, q in ((6, q_c), (7, q_b), (8, q_a)):
        load_items.append(load(index, items_hbm.at[rows(q)], items.at[rows(q)]))
    load_noise_users = load(9, noise_users_hbm, noise_users)
    load_noise_items = [load(10, noise_items_hbm.at[0, rows(q_a)], noise_items.at[0]),
                        load(11, noise_items_hbm.at[1, rows(q_c)], noise_items.at[1])]

    def remote(kind, k, source, target, device):
        return pltpu.make_async_remote_copy(
            src_ref=source, dst_ref=target, send_sem=send_sem.at[kind, k],
            recv_sem=recv_sem.at[kind, k], device_id=device, device_id_type=MESH)

    def copy_of(kind, k):
        size = chunk(kind)
        piece = pl.ds(k * size, size)
        s = 0 if kind < S1_SIB_FAR else 1
        if kind in (S0_SIB_FAR, S1_SIB_FAR):
            return remote(kind, k, part.at[s, 0, piece], from_sib_far.at[s, piece], sibling)
        if kind in (S0_X, S1_X):
            return remote(kind, k, part.at[s, 1, piece], from_x.at[s, piece], across)
        if kind in (S0_SIB_OWN, S1_SIB_OWN):
            return remote(kind, k, part.at[s, 2, piece], from_sib_own.at[s, piece], sibling)
        if kind == FORWARD:
            return remote(kind, k, moved.at[0, piece], position.at[rows(q_a, k * size, size)], ahead)
        if kind == FINAL:
            return remote(kind, k, moved.at[1, piece], items_out.at[piece], ahead)
        where = rows(q_c if kind == RELAY_LAST else q_a, k * size, size)
        other = across if kind == RELAY_X else sibling
        return remote(kind, k, position.at[where], position.at[where], other)

    def send(kind, k):
        copy_of(kind, k).start()

    def arrive(kind, k):
        copy_of(kind, k).wait_recv()

    def cell(stratum, row, column):
        wanted = row * item_tiles + column
        slot = jnp.int32(0)
        live = jnp.float32(0)
        for s in range(slots):
            hit = jnp.logical_and(tiles[stratum, s] == wanted, s < counts[0, stratum])
            slot = jnp.where(hit, s, slot)
            live = jnp.where(hit, jnp.float32(1), live)
        return (ratings[stratum, slot].astype(F32), weights[stratum, slot].astype(F32) * live)

    def grads(stratum, place, q, target):
        item_rows = blocks[stratum, rows(q), :]
        predicted = dot(u_wide[...], right_triple(item_rows, 1), ((1,), (1,)))
        v_tall[place] = right_triple(item_rows, 0)
        bands = []
        for r in range(per):
            line = []
            for j in range(per):
                rating, weight = cell(stratum, r, q * per + j)
                line.append(weight * (rating - predicted[r * TILE:(r + 1) * TILE, j * TILE:(j + 1) * TILE]))
            bands.append(jnp.concatenate(line, axis=1))
        err = jnp.concatenate(bands, axis=0)
        e_wide[place] = left_triple(err, 1)
        part[stratum, target] = dot(left_triple(err.T, 1), u_tall[...], ((1,), (0,)))

    def send_far(stratum, j):
        span = slice(j * TILE, (j + 1) * TILE)
        arrive((S0_SIB_FAR, S1_SIB_FAR)[stratum], j)
        part[stratum, 1, span] += from_sib_far[stratum, span]
        kind = (S0_X, S1_X)[stratum]
        for k in range(j * FINE // per, (j + 1) * FINE // per):
            send(kind, k)

    def split_users():
        now = users[...]
        u_wide[...] = left_triple(now, 1)
        u_tall[...] = right_triple(now, 0)

    def user_step(stratum):
        now = users[...]
        total = dot(jnp.concatenate([e_wide[p] for p in range(4)], axis=1),
                    jnp.concatenate([v_tall[p] for p in range(4)], axis=0), ((1,), (0,)))
        users[...] = now + STEP_SIZE * (LIKELIHOOD * total - now) + NOISE_SCALE * noise_users[stratum]

    def item_step(stratum, now, k):
        piece = pl.ds(k * quarter // FINE, quarter // FINE)
        arrive((S0_X, S1_X)[stratum], k)
        total = part[stratum, 3, piece] + from_sib_own[stratum, piece] + from_x[stratum, piece]
        moved[stratum, piece] = (now + STEP_SIZE * (LIKELIHOOD * total - now)
                                 + NOISE_SCALE * noise_items[stratum, piece])
        send((FORWARD, FINAL)[stratum], k)

    def relay(k):
        arrive(FORWARD, k)
        send(RELAY_X, k)
        if (k + 1) * per % FINE == 0:
            send(RELAY_SIB, (k + 1) * per // FINE - 1)

    def finish(stratum, q):
        fine = quarter // FINE
        for k in range(FINE):
            if k * per % FINE == 0:
                arrive((S0_SIB_OWN, S1_SIB_OWN)[stratum], k * per // FINE)
            item_step(stratum, blocks[stratum, rows(q, k * fine, fine), :], k)
            if stratum == 0 and k >= 2:
                relay(k - 2)

    def send_all(kind):
        for j in range(count(kind)):
            send(kind, j)

    def arrive_all(kind):
        for j in range(count(kind)):
            arrive(kind, j)

    load_users.wait()
    split_users()
    load_tiles.wait()
    load_counts.wait()
    load_ratings.wait()
    load_weights.wait()
    pl.semaphore_wait(barrier, 4)

    def step(i, carry):
        stratum = i // 4
        place = i % 4
        q = jnp.where(jnp.logical_or(i == 0, i == 7), q_d,
                      jnp.where(jnp.logical_or(i == 1, i == 6), q_c,
                                jnp.where(jnp.logical_or(i == 2, i == 4), q_b, q_a)))
        target = jnp.where(i < 6, place, 9 - i)
        for p in range(4):
            @pl.when(i == p)
            def _():
                load_items[p].wait()

        @pl.when(i == 4)
        def _():
            for k in range(FINE - 2, FINE):
                relay(k)
            arrive_all(RELAY_SIB)

        @pl.when(i == 6)
        def _():
            arrive_all(RELAY_X)
            send_all(RELAY_LAST)

        @pl.when(i == 7)
        def _():
            arrive_all(RELAY_LAST)

        grads(stratum, place, q, target)

        @pl.when(i == 0)
        def _():
            send_all(S0_SIB_FAR)

        @pl.when(i == 1)
        def _():
            for j in range(per):
                send_far(0, j)

        @pl.when(i == 2)
        def _():
            send_all(S0_SIB_OWN)

        @pl.when(i == 4)
        def _():
            send_all(S1_SIB_FAR)

        @pl.when(i == 5)
        def _():
            for j in range(per):
                send_far(1, j)

        @pl.when(i == 7)
        def _():
            send_all(S1_SIB_OWN)

        @pl.when(i == 3)
        def _():
            load_noise_users.wait()

        @pl.when(place == 3)
        def _():
            user_step(stratum)

        @pl.when(i == 3)
        def _():
            split_users()
            for late in load_noise_items:
                late.wait()
            finish(0, q_a)

        return carry

    lax.fori_loop(0, 8, step, 0)
    store = pltpu.make_async_copy(users, users_out, out_sem)
    store.start()
    finish(1, q_c)
    for kind in range(KINDS):
        for k in range(count(kind)):
            copy_of(kind, k).wait_send()
    store.wait()
    arrive_all(FINAL)


def body(n_blk, users, items, noise_users, noise_items, tile_index, counts, ratings, weights):
    mine, rank = users.shape
    slots, tile = ratings.shape[1], ratings.shape[2]
    kept = (mine, rank)
    any_spec = pl.BlockSpec(memory_space=pl.ANY)
    work = 2 * 3 * 3 * 2 * mine * items.shape[0] * rank
    return pl.pallas_call(
        functools.partial(kernel, n_blk),
        out_shape=(pltpu.VMEM(kept, F32), pltpu.VMEM(kept, F32)),
        in_specs=[any_spec] * 8,
        out_specs=(any_spec, any_spec),
        scratch_shapes=[
            pltpu.SMEM(tile_index.shape, jnp.int32),
            pltpu.SMEM((1, counts.shape[0]), jnp.int32),
            pltpu.VMEM(kept, F32),
            pltpu.VMEM((2,) + items.shape, F32),
            pltpu.VMEM((2,) + kept, F32),
            pltpu.VMEM((2,) + kept, F32),
            pltpu.VMEM((2, slots, tile, tile), BF16),
            pltpu.VMEM((2, slots, tile, tile), BF16),
            pltpu.VMEM((mine, 3 * rank), BF16),
            pltpu.VMEM((3 * mine, rank), BF16),
            pltpu.VMEM((4, 3 * mine, rank), BF16),
            pltpu.VMEM((4, mine, 3 * mine), BF16),
            pltpu.VMEM((2, 4) + kept, F32),
            pltpu.VMEM((2,) + kept, F32),
            pltpu.VMEM((2,) + kept, F32),
            pltpu.VMEM((2,) + kept, F32),
            pltpu.VMEM((2,) + kept, F32),
            pltpu.SemaphoreType.DMA((12,)),
            pltpu.SemaphoreType.DMA,
            pltpu.SemaphoreType.DMA((KINDS, FINE)),
            pltpu.SemaphoreType.DMA((KINDS, FINE)),
        ],
        compiler_params=pltpu.CompilerParams(
            collective_id=0, has_side_effects=True, vmem_limit_bytes=56 * 1024 * 1024),
        cost_estimate=pl.CostEstimate(flops=work, bytes_accessed=4 * 2 ** 20, transcendentals=0),
    )(tile_index, counts.T, users, items, noise_users, noise_items, ratings, weights)


def solution(mesh):
    in_specs = (
        P(("blk", "grp"), None),
        P("blk", None),
        P(None, ("blk", "grp"), None),
        P(None, "blk", None),
        P(None, ("blk", "grp")),
        P(None, ("blk", "grp")),
        P(None, ("blk", "grp"), None, None),
        P(None, ("blk", "grp"), None, None),
    )
    out_specs = (P(("blk", "grp"), None), P(("blk", "grp"), None))
    return jax.shard_map(functools.partial(body, mesh.shape["blk"]), mesh=mesh,
                         in_specs=in_specs, out_specs=out_specs, check_vma=False)
```

```python
import functools
import math

import jax
import jax.numpy as jnp
from jax import lax
from jax.experimental import pallas as pl
from jax.experimental.pallas import tpu as pltpu
from jax.sharding import PartitionSpec as P

STEP_SIZE = 0.001
LIKELIHOOD = 20.0
NOISE_SCALE = math.sqrt(0.002)
TILE = 128
FINE = 4
MESH = pl.DeviceIdType.MESH
F32 = jnp.float32
BF16 = jnp.bfloat16

(S0_SIB_FAR, S0_X, S0_SIB_OWN, FORWARD, RELAY_SIB, RELAY_X, RELAY_LAST,
 S1_SIB_FAR, S1_X, S1_SIB_OWN, FINAL) = range(11)
KINDS = 11
ON_CHIP = (S0_SIB_FAR, S0_SIB_OWN, RELAY_SIB, RELAY_LAST, S1_SIB_FAR, S1_SIB_OWN)


def halves(value):
    high = value.astype(BF16)
    low = (value - high.astype(F32)).astype(BF16)
    return high, low


def dot(left, right, contract):
    return lax.dot_general(left, right, (contract, ((), ())), preferred_element_type=F32)


def left_triple(value, axis):
    high, low = halves(value)
    return jnp.concatenate([high, low, high], axis=axis)


def right_triple(value, axis):
    high, low = halves(value)
    return jnp.concatenate([high, high, low], axis=axis)


def kernel(n_blk, tiles_hbm, counts_hbm, users_hbm, items_hbm, noise_users_hbm, noise_items_hbm,
           ratings_hbm, weights_hbm, users_out, items_out,
           tiles, counts, table, users, blocks, noise_users, noise_items, ratings, weights,
           u_wide, u_tall, v_tall, e_wide, part, from_sib_far, from_x,
           from_sib_own, moved, local_sem, out_sem, send_sem, recv_sem):
    quarter = users.shape[0]
    per = quarter // TILE
    items = blocks.at[0]
    position = blocks.at[1]
    item_tiles = items.shape[0] // TILE
    slots = tiles.shape[1]
    blk = lax.axis_index("blk")
    grp = lax.axis_index("grp")
    side = grp // 2
    core = grp % 2
    sibling = (blk, side * 2 + (1 - core))
    across = (blk, (1 - side) * 2 + core)
    ahead = ((blk + 1) % n_blk, grp)
    behind = ((blk + n_blk - 1) % n_blk, grp)
    q_a = (1 - side) * 2 + core
    q_b = (1 - side) * 2 + (1 - core)
    q_c = side * 2 + core
    q_d = side * 2 + (1 - core)

    def rows(q, start=0, size=quarter):
        return pl.ds(pl.multiple_of(q * quarter + start, size), size)

    def chunk(kind):
        return TILE if kind in ON_CHIP else quarter // FINE

    def count(kind):
        return quarter // chunk(kind)

    def load(index, source, target):
        copy = pltpu.make_async_copy(source, target, local_sem.at[index])
        copy.start()
        return copy

    load_tiles = load(0, tiles_hbm, tiles)
    load_counts = load(1, counts_hbm, counts)
    load_users = load(2, users_hbm, users)
    load_items = [load(3, items_hbm.at[rows(q_d)], items.at[rows(q_d)])]
    load_ratings = load(4, ratings_hbm, ratings)
    load_weights = load(5, weights_hbm, weights)
    barrier = pltpu.get_barrier_semaphore()
    for other in (sibling, across, ahead, behind):
        pl.semaphore_signal(barrier, inc=1, device_id=other, device_id_type=MESH)
    for index, q in ((6, q_c), (7, q_b), (8, q_a)):
        load_items.append(load(index, items_hbm.at[rows(q)], items.at[rows(q)]))
    load_noise_users = load(9, noise_users_hbm, noise_users)
    load_noise_items = [load(10, noise_items_hbm.at[0, rows(q_a)], noise_items.at[0]),
                        load(11, noise_items_hbm.at[1, rows(q_c)], noise_items.at[1])]

    def remote(kind, k, source, target, device):
        return pltpu.make_async_remote_copy(
            src_ref=source, dst_ref=target, send_sem=send_sem.at[kind, k],
            recv_sem=recv_sem.at[kind, k], device_id=device, device_id_type=MESH)

    def copy_of(kind, k):
        size = chunk(kind)
        piece = pl.ds(k * size, size)
        s = 0 if kind < S1_SIB_FAR else 1
        if kind in (S0_SIB_FAR, S1_SIB_FAR):
            return remote(kind, k, part.at[s, 0, piece], from_sib_far.at[s, piece], sibling)
        if kind in (S0_X, S1_X):
            return remote(kind, k, part.at[s, 1, piece], from_x.at[s, piece], across)
        if kind in (S0_SIB_OWN, S1_SIB_OWN):
            return remote(kind, k, part.at[s, 2, piece], from_sib_own.at[s, piece], sibling)
        if kind == FORWARD:
            return remote(kind, k, moved.at[0, piece], position.at[rows(q_a, k * size, size)], ahead)
        if kind == FINAL:
            return remote(kind, k, moved.at[1, piece], items_out.at[piece], ahead)
        where = rows(q_c if kind == RELAY_LAST else q_a, k * size, size)
        other = across if kind == RELAY_X else sibling
        return remote(kind, k, position.at[where], position.at[where], other)

    def send(kind, k):
        copy_of(kind, k).start()

    def arrive(kind, k):
        copy_of(kind, k).wait_recv()

    def fill_table(i, carry):
        stratum = i // (per * item_tiles)
        wanted = i % (per * item_tiles)
        slot = jnp.int32(-1)
        for s in range(slots):
            hit = jnp.logical_and(tiles[stratum, s] == wanted, s < counts[0, stratum])
            slot = jnp.where(hit, s, slot)
        table[i] = slot
        return carry

    def cell_err(stratum, row, column, predicted):
        slot = table[(stratum * per + row) * item_tiles + column]
        live = jnp.where(slot >= 0, jnp.float32(1), jnp.float32(0))
        slot = jnp.maximum(slot, 0)
        weight = weights[stratum, slot].astype(F32) * live
        return weight * (ratings[stratum, slot].astype(F32) - predicted)

    def grads(stratum, place, q, start, size):
        item_rows = blocks[stratum, rows(q, start, size), :]
        predicted = dot(u_wide[...], right_triple(item_rows, 1), ((1,), (1,)))
        bands = []
        for r in range(per):
            line = []
            for j in range(size // TILE):
                column = q * per + start // TILE + j
                line.append(cell_err(stratum, r, column,
                                     predicted[r * TILE:(r + 1) * TILE, j * TILE:(j + 1) * TILE]))
            bands.append(jnp.concatenate(line, axis=1))
        err = jnp.concatenate(bands, axis=0)
        part[stratum, place, pl.ds(start, size)] = dot(left_triple(err.T, 1), u_tall[...], ((1,), (0,)))
        item_high, item_low = halves(item_rows)
        err_high, err_low = halves(err)
        for third, item_part, err_part in ((0, item_high, err_high), (1, item_high, err_low),
                                           (2, item_low, err_high)):
            span = pl.ds(pl.multiple_of(third * quarter + start, size), size)
            v_tall[place, span] = item_part
            e_wide[place, :, span] = err_part

    def send_far(stratum, j):
        span = slice(j * TILE, (j + 1) * TILE)
        arrive((S0_SIB_FAR, S1_SIB_FAR)[stratum], j)
        part[stratum, 1, span] += from_sib_far[stratum, span]
        kind = (S0_X, S1_X)[stratum]
        for k in range(j * FINE // per, (j + 1) * FINE // per):
            send(kind, k)

    def split_users():
        now = users[...]
        u_wide[...] = left_triple(now, 1)
        u_tall[...] = right_triple(now, 0)

    def user_step(stratum):
        now = users[...]
        total = dot(jnp.concatenate([e_wide[p] for p in range(4)], axis=1),
                    jnp.concatenate([v_tall[p] for p in range(4)], axis=0), ((1,), (0,)))
        users[...] = now + STEP_SIZE * (LIKELIHOOD * total - now) + NOISE_SCALE * noise_users[stratum]

    def item_step(stratum, now, k):
        piece = pl.ds(k * quarter // FINE, quarter // FINE)
        arrive((S0_X, S1_X)[stratum], k)
        total = part[stratum, 3, piece] + from_sib_own[stratum, piece] + from_x[stratum, piece]
        moved[stratum, piece] = (now + STEP_SIZE * (LIKELIHOOD * total - now)
                                 + NOISE_SCALE * noise_items[stratum, piece])
        send((FORWARD, FINAL)[stratum], k)

    def relay(k):
        arrive(FORWARD, k)
        send(RELAY_X, k)
        if (k + 1) * per % FINE == 0:
            send(RELAY_SIB, (k + 1) * per // FINE - 1)

    def finish(stratum, q, k):
        fine = quarter // FINE
        if k * per % FINE == 0:
            arrive((S0_SIB_OWN, S1_SIB_OWN)[stratum], k * per // FINE)
        item_step(stratum, blocks[stratum, rows(q, k * fine, fine), :], k)

    def send_all(kind):
        for j in range(count(kind)):
            send(kind, j)

    def arrive_all(kind):
        for j in range(count(kind)):
            arrive(kind, j)

    load_tiles.wait()
    load_counts.wait()
    lax.fori_loop(0, 2 * per * item_tiles, fill_table, 0)
    load_users.wait()
    split_users()
    load_ratings.wait()
    load_weights.wait()
    pl.semaphore_wait(barrier, 4)

    def first(i, carry):
        for p in range(4):
            @pl.when(i == p)
            def _():
                load_items[p].wait()

        grads(0, i, jnp.where(i == 0, q_d, jnp.where(i == 1, q_c, jnp.where(i == 2, q_b, q_a))), 0, quarter)

        @pl.when(i == 0)
        def _():
            send_all(S0_SIB_FAR)

        @pl.when(i == 1)
        def _():
            for j in range(per):
                send_far(0, j)

        @pl.when(i == 2)
        def _():
            send_all(S0_SIB_OWN)

        return carry

    lax.fori_loop(0, 4, first, 0)
    load_noise_items[0].wait()
    finish(0, q_a, 0)
    load_noise_users.wait()
    user_step(0)
    split_users()
    for k in range(1, FINE):
        finish(0, q_a, k)
        if k >= 2:
            relay(k - 2)

    def second(i, carry):
        place = jnp.where(i < 4, i % 2, 3 - (i - 4) // 2)
        j = jnp.where(i < 4, i // 2, i % 2)
        q = jnp.where(place == 0, q_b, jnp.where(place == 1, q_a, jnp.where(place == 2, q_d, q_c)))
        for n in range(per):
            @pl.when(i == 2 * n)
            def _():
                arrive(RELAY_SIB, n)

            @pl.when(i == 6 + n)
            def _():
                arrive(RELAY_LAST, n)

            @pl.when(i == 4 + n)
            def _():
                for k in range(n * FINE // per, (n + 1) * FINE // per):
                    arrive(RELAY_X, k)
                send(RELAY_LAST, n)

        grads(1, place, q, pl.multiple_of(j * TILE, TILE), TILE)
        for n in range(per):
            @pl.when(i == 2 * n)
            def _():
                send(S1_SIB_FAR, n)

            @pl.when(i == 2 * n + 1)
            def _():
                send_far(1, n)

            @pl.when(i == 6 + n)
            def _():
                send(S1_SIB_OWN, n)

            @pl.when(i == n)
            def _():
                for k in range(FINE - 2 + n * 2 // per, FINE - 2 + (n + 1) * 2 // per):
                    relay(k)

        return carry

    lax.fori_loop(0, 8, second, 0)
    user_step(1)
    store = pltpu.make_async_copy(users, users_out, out_sem)
    store.start()
    load_noise_items[1].wait()
    for k in range(FINE):
        finish(1, q_c, k)
    for kind in range(KINDS):
        for k in range(count(kind)):
            copy_of(kind, k).wait_send()
    store.wait()
    arrive_all(FINAL)


def body(n_blk, users, items, noise_users, noise_items, tile_index, counts, ratings, weights):
    mine, rank = users.shape
    slots, tile = ratings.shape[1], ratings.shape[2]
    kept = (mine, rank)
    any_spec = pl.BlockSpec(memory_space=pl.ANY)
    work = 2 * 3 * 3 * 2 * mine * items.shape[0] * rank
    return pl.pallas_call(
        functools.partial(kernel, n_blk),
        out_shape=(pltpu.VMEM(kept, F32), pltpu.VMEM(kept, F32)),
        in_specs=[any_spec] * 8,
        out_specs=(any_spec, any_spec),
        scratch_shapes=[
            pltpu.SMEM(tile_index.shape, jnp.int32),
            pltpu.SMEM((1, counts.shape[0]), jnp.int32),
            pltpu.SMEM((2 * (mine // tile) * (items.shape[0] // tile),), jnp.int32),
            pltpu.VMEM(kept, F32),
            pltpu.VMEM((2,) + items.shape, F32),
            pltpu.VMEM((2,) + kept, F32),
            pltpu.VMEM((2,) + kept, F32),
            pltpu.VMEM((2, slots, tile, tile), BF16),
            pltpu.VMEM((2, slots, tile, tile), BF16),
            pltpu.VMEM((mine, 3 * rank), BF16),
            pltpu.VMEM((3 * mine, rank), BF16),
            pltpu.VMEM((4, 3 * mine, rank), BF16),
            pltpu.VMEM((4, mine, 3 * mine), BF16),
            pltpu.VMEM((2, 4) + kept, F32),
            pltpu.VMEM((2,) + kept, F32),
            pltpu.VMEM((2,) + kept, F32),
            pltpu.VMEM((2,) + kept, F32),
            pltpu.VMEM((2,) + kept, F32),
            pltpu.SemaphoreType.DMA((12,)),
            pltpu.SemaphoreType.DMA,
            pltpu.SemaphoreType.DMA((KINDS, FINE)),
            pltpu.SemaphoreType.DMA((KINDS, FINE)),
        ],
        compiler_params=pltpu.CompilerParams(
            collective_id=0, has_side_effects=True, vmem_limit_bytes=56 * 1024 * 1024),
        cost_estimate=pl.CostEstimate(flops=work, bytes_accessed=4 * 2 ** 20, transcendentals=0),
    )(tile_index, counts.T, users, items, noise_users, noise_items, ratings, weights)


def solution(mesh):
    in_specs = (
        P(("blk", "grp"), None),
        P("blk", None),
        P(None, ("blk", "grp"), None),
        P(None, "blk", None),
        P(None, ("blk", "grp")),
        P(None, ("blk", "grp")),
        P(None, ("blk", "grp"), None, None),
        P(None, ("blk", "grp"), None, None),
    )
    out_specs = (P(("blk", "grp"), None), P(("blk", "grp"), None))
    return jax.shard_map(functools.partial(body, mesh.shape["blk"]), mesh=mesh,
                         in_specs=in_specs, out_specs=out_specs, check_vma=False)
```

```python
import functools
import math

import jax
import jax.numpy as jnp
from jax import lax
from jax.experimental import pallas as pl
from jax.experimental.pallas import tpu as pltpu
from jax.sharding import PartitionSpec as P

STEP_SIZE = 0.001
LIKELIHOOD = 20.0
NOISE_SCALE = math.sqrt(0.002)
TILE = 128
FINE = 4
MESH = pl.DeviceIdType.MESH
F32 = jnp.float32
BF16 = jnp.bfloat16

(S0_SIB_FAR, S0_X, S0_SIB_OWN, FORWARD, RELAY_SIB, RELAY_X, RELAY_LAST,
 S1_SIB_FAR, S1_X, S1_SIB_OWN, FINAL) = range(11)
KINDS = 11
ON_CHIP = (S0_SIB_FAR, S0_SIB_OWN, RELAY_SIB, RELAY_LAST, S1_SIB_FAR, S1_SIB_OWN)


def halves(value):
    high = value.astype(BF16)
    low = (value - high.astype(F32)).astype(BF16)
    return high, low


def dot(left, right, contract):
    return lax.dot_general(left, right, (contract, ((), ())), preferred_element_type=F32)


def left_triple(value, axis):
    high, low = halves(value)
    return jnp.concatenate([high, low, high], axis=axis)


def right_triple(value, axis):
    high, low = halves(value)
    return jnp.concatenate([high, high, low], axis=axis)


def kernel(n_blk, tiles_hbm, counts_hbm, users_hbm, items_hbm, noise_users_hbm, noise_items_hbm,
           ratings_hbm, weights_hbm, users_out, items_out,
           tiles, counts, table, users, blocks, noise_users, noise_items, ratings, weights,
           ratings_t, weights_t, ut_tall, u_tall, v_tall, err_t, part, from_sib_far, from_x,
           from_sib_own, moved, local_sem, out_sem, send_sem, recv_sem):
    quarter = users.shape[0]
    per = quarter // TILE
    items = blocks.at[0]
    position = blocks.at[1]
    item_tiles = items.shape[0] // TILE
    slots = tiles.shape[1]
    blk = lax.axis_index("blk")
    grp = lax.axis_index("grp")
    side = grp // 2
    core = grp % 2
    sibling = (blk, side * 2 + (1 - core))
    across = (blk, (1 - side) * 2 + core)
    ahead = ((blk + 1) % n_blk, grp)
    behind = ((blk + n_blk - 1) % n_blk, grp)
    q_a = (1 - side) * 2 + core
    q_b = (1 - side) * 2 + (1 - core)
    q_c = side * 2 + core
    q_d = side * 2 + (1 - core)

    def rows(q, start=0, size=quarter):
        return pl.ds(pl.multiple_of(q * quarter + start, size), size)

    def chunk(kind):
        return TILE if kind in ON_CHIP else quarter // FINE

    def count(kind):
        return quarter // chunk(kind)

    def load(index, source, target):
        copy = pltpu.make_async_copy(source, target, local_sem.at[index])
        copy.start()
        return copy

    load_tiles = load(0, tiles_hbm, tiles)
    load_counts = load(1, counts_hbm, counts)
    load_users = load(2, users_hbm, users)
    load_items = [load(3, items_hbm.at[rows(q_d)], items.at[rows(q_d)])]
    load_ratings = load(4, ratings_hbm, ratings)
    load_weights = load(5, weights_hbm, weights)
    barrier = pltpu.get_barrier_semaphore()
    for other in (sibling, across, ahead, behind):
        pl.semaphore_signal(barrier, inc=1, device_id=other, device_id_type=MESH)
    for index, q in ((6, q_c), (7, q_b), (8, q_a)):
        load_items.append(load(index, items_hbm.at[rows(q)], items.at[rows(q)]))
    load_noise_users = load(9, noise_users_hbm, noise_users)
    load_noise_items = [load(10, noise_items_hbm.at[0, rows(q_a)], noise_items.at[0]),
                        load(11, noise_items_hbm.at[1, rows(q_c)], noise_items.at[1])]

    def remote(kind, k, source, target, device):
        return pltpu.make_async_remote_copy(
            src_ref=source, dst_ref=target, send_sem=send_sem.at[kind, k],
            recv_sem=recv_sem.at[kind, k], device_id=device, device_id_type=MESH)

    def copy_of(kind, k):
        size = chunk(kind)
        piece = pl.ds(k * size, size)
        s = 0 if kind < S1_SIB_FAR else 1
        if kind in (S0_SIB_FAR, S1_SIB_FAR):
            return remote(kind, k, part.at[s, 0, piece], from_sib_far.at[s, piece], sibling)
        if kind in (S0_X, S1_X):
            return remote(kind, k, part.at[s, 1, piece], from_x.at[s, piece], across)
        if kind in (S0_SIB_OWN, S1_SIB_OWN):
            return remote(kind, k, part.at[s, 2, piece], from_sib_own.at[s, piece], sibling)
        if kind == FORWARD:
            return remote(kind, k, moved.at[0, piece], position.at[rows(q_a, k * size, size)], ahead)
        if kind == FINAL:
            return remote(kind, k, moved.at[1, piece], items_out.at[piece], ahead)
        where = rows(q_c if kind == RELAY_LAST else q_a, k * size, size)
        other = across if kind == RELAY_X else sibling
        return remote(kind, k, position.at[where], position.at[where], other)

    def send(kind, k):
        copy_of(kind, k).start()

    def arrive(kind, k):
        copy_of(kind, k).wait_recv()

    def fill_table(i, carry):
        stratum = i // (per * item_tiles)
        wanted = i % (per * item_tiles)
        slot = jnp.int32(-1)
        for s in range(slots):
            hit = jnp.logical_and(tiles[stratum, s] == wanted, s < counts[0, stratum])
            slot = jnp.where(hit, s, slot)
        table[i] = slot
        return carry

    def cell_err(stratum, row, column, predicted):
        slot = table[(stratum * per + row) * item_tiles + column]
        live = jnp.where(slot >= 0, jnp.float32(1), jnp.float32(0))
        slot = jnp.maximum(slot, 0)
        weight = weights_t[stratum, slot].astype(F32) * live
        return weight * (ratings_t[stratum, slot].astype(F32) - predicted)

    def turn_tiles(stratum):
        def turn(i, carry):
            ratings_t[stratum, i] = ratings[stratum, i].T
            weights_t[stratum, i] = weights[stratum, i].T
            return carry

        lax.fori_loop(0, slots, turn, 0)

    def grads(stratum, place, q, start, size):
        item_rows = blocks[stratum, rows(q, start, size), :]
        predicted = dot(left_triple(item_rows, 1), ut_tall[...], ((1,), (0,)))
        bands = []
        for j in range(size // TILE):
            column = q * per + start // TILE + j
            line = []
            for r in range(per):
                line.append(cell_err(stratum, r, column,
                                     predicted[j * TILE:(j + 1) * TILE, r * TILE:(r + 1) * TILE]))
            bands.append(jnp.concatenate(line, axis=1))
        err = jnp.concatenate(bands, axis=0)
        part[stratum, place, pl.ds(start, size)] = dot(left_triple(err, 1), u_tall[...], ((1,), (0,)))
        err_t[place, pl.ds(start, size)] = err
        item_high, item_low = halves(item_rows)
        for third, item_part in ((0, item_high), (1, item_high), (2, item_low)):
            v_tall[place, pl.ds(pl.multiple_of(third * quarter + start, size), size)] = item_part

    def send_far(stratum, j):
        span = slice(j * TILE, (j + 1) * TILE)
        arrive((S0_SIB_FAR, S1_SIB_FAR)[stratum], j)
        part[stratum, 1, span] += from_sib_far[stratum, span]
        kind = (S0_X, S1_X)[stratum]
        for k in range(j * FINE // per, (j + 1) * FINE // per):
            send(kind, k)

    def split_users():
        now = users[...]
        ut_tall[...] = right_triple(now.T, 0)
        u_tall[...] = right_triple(now, 0)

    def user_step(stratum):
        now = users[...]
        total = jnp.zeros(now.shape, F32)
        for p in range(4):
            total += dot(left_triple(err_t[p].T, 1), v_tall[p], ((1,), (0,)))
        users[...] = now + STEP_SIZE * (LIKELIHOOD * total - now) + NOISE_SCALE * noise_users[stratum]

    def item_step(stratum, now, k):
        piece = pl.ds(k * quarter // FINE, quarter // FINE)
        arrive((S0_X, S1_X)[stratum], k)
        total = part[stratum, 3, piece] + from_sib_own[stratum, piece] + from_x[stratum, piece]
        moved[stratum, piece] = (now + STEP_SIZE * (LIKELIHOOD * total - now)
                                 + NOISE_SCALE * noise_items[stratum, piece])
        send((FORWARD, FINAL)[stratum], k)

    def relay(k):
        arrive(FORWARD, k)
        send(RELAY_X, k)
        if (k + 1) * per % FINE == 0:
            send(RELAY_SIB, (k + 1) * per // FINE - 1)

    def finish(stratum, q, k):
        fine = quarter // FINE
        if k * per % FINE == 0:
            arrive((S0_SIB_OWN, S1_SIB_OWN)[stratum], k * per // FINE)
        item_step(stratum, blocks[stratum, rows(q, k * fine, fine), :], k)

    def send_all(kind):
        for j in range(count(kind)):
            send(kind, j)

    def arrive_all(kind):
        for j in range(count(kind)):
            arrive(kind, j)

    load_tiles.wait()
    load_counts.wait()
    lax.fori_loop(0, 2 * per * item_tiles, fill_table, 0)
    load_users.wait()
    split_users()
    load_ratings.wait()
    load_weights.wait()
    turn_tiles(0)
    pl.semaphore_wait(barrier, 4)

    def first(i, carry):
        for p in range(4):
            @pl.when(i == p)
            def _():
                load_items[p].wait()

        grads(0, i, jnp.where(i == 0, q_d, jnp.where(i == 1, q_c, jnp.where(i == 2, q_b, q_a))), 0, quarter)

        @pl.when(i == 0)
        def _():
            send_all(S0_SIB_FAR)

        @pl.when(i == 1)
        def _():
            for j in range(per):
                send_far(0, j)

        @pl.when(i == 2)
        def _():
            send_all(S0_SIB_OWN)

        return carry

    lax.fori_loop(0, 4, first, 0)
    load_noise_items[0].wait()
    finish(0, q_a, 0)
    load_noise_users.wait()
    user_step(0)
    split_users()
    for k in range(1, FINE):
        finish(0, q_a, k)
        if k == 1:
            turn_tiles(1)
        if k >= 2:
            relay(k - 2)

    def second(i, carry):
        place = i % 2
        for n in range(per):
            @pl.when(i == 2 * n)
            def _():
                arrive(RELAY_SIB, n)

        grads(1, place, jnp.where(place == 0, q_b, q_a), pl.multiple_of(i // 2 * TILE, TILE), TILE)
        for n in range(per):
            @pl.when(i == 2 * n)
            def _():
                send(S1_SIB_FAR, n)

            @pl.when(i == n)
            def _():
                for k in range(FINE - 2 + n * 2 // per, FINE - 2 + (n + 1) * 2 // per):
                    relay(k)

            @pl.when(i == 2 * n + 1)
            def _():
                send_far(1, n)

        return carry

    lax.fori_loop(0, 2 * per, second, 0)

    def third(i, carry):
        @pl.when(i == 0)
        def _():
            for n in range(per):
                for k in range(n * FINE // per, (n + 1) * FINE // per):
                    arrive(RELAY_X, k)
                send(RELAY_LAST, n)

        @pl.when(i == 1)
        def _():
            arrive_all(RELAY_LAST)

        grads(1, 3 - i, jnp.where(i == 0, q_c, q_d), 0, quarter)

        @pl.when(i == 1)
        def _():
            send_all(S1_SIB_OWN)

        return carry

    lax.fori_loop(0, 2, third, 0)
    load_noise_items[1].wait()
    for k in range(FINE):
        finish(1, q_c, k)
    user_step(1)
    store = pltpu.make_async_copy(users, users_out, out_sem)
    store.start()
    for kind in range(KINDS):
        for k in range(count(kind)):
            copy_of(kind, k).wait_send()
    store.wait()
    arrive_all(FINAL)


def body(n_blk, users, items, noise_users, noise_items, tile_index, counts, ratings, weights):
    mine, rank = users.shape
    slots, tile = ratings.shape[1], ratings.shape[2]
    kept = (mine, rank)
    any_spec = pl.BlockSpec(memory_space=pl.ANY)
    work = 2 * 3 * 3 * 2 * mine * items.shape[0] * rank
    return pl.pallas_call(
        functools.partial(kernel, n_blk),
        out_shape=(pltpu.VMEM(kept, F32), pltpu.VMEM(kept, F32)),
        in_specs=[any_spec] * 8,
        out_specs=(any_spec, any_spec),
        scratch_shapes=[
            pltpu.SMEM(tile_index.shape, jnp.int32),
            pltpu.SMEM((1, counts.shape[0]), jnp.int32),
            pltpu.SMEM((2 * (mine // tile) * (items.shape[0] // tile),), jnp.int32),
            pltpu.VMEM(kept, F32),
            pltpu.VMEM((2,) + items.shape, F32),
            pltpu.VMEM((2,) + kept, F32),
            pltpu.VMEM((2,) + kept, F32),
            pltpu.VMEM((2, slots, tile, tile), BF16),
            pltpu.VMEM((2, slots, tile, tile), BF16),
            pltpu.VMEM((2, slots, tile, tile), BF16),
            pltpu.VMEM((2, slots, tile, tile), BF16),
            pltpu.VMEM((3 * rank, mine), BF16),
            pltpu.VMEM((3 * mine, rank), BF16),
            pltpu.VMEM((4, 3 * mine, rank), BF16),
            pltpu.VMEM((4, mine, mine), F32),
            pltpu.VMEM((2, 4) + kept, F32),
            pltpu.VMEM((2,) + kept, F32),
            pltpu.VMEM((2,) + kept, F32),
            pltpu.VMEM((2,) + kept, F32),
            pltpu.VMEM((2,) + kept, F32),
            pltpu.SemaphoreType.DMA((12,)),
            pltpu.SemaphoreType.DMA,
            pltpu.SemaphoreType.DMA((KINDS, FINE)),
            pltpu.SemaphoreType.DMA((KINDS, FINE)),
        ],
        compiler_params=pltpu.CompilerParams(
            collective_id=0, has_side_effects=True, vmem_limit_bytes=56 * 1024 * 1024),
        cost_estimate=pl.CostEstimate(flops=work, bytes_accessed=4 * 2 ** 20, transcendentals=0),
    )(tile_index, counts.T, users, items, noise_users, noise_items, ratings, weights)


def solution(mesh):
    in_specs = (
        P(("blk", "grp"), None),
        P("blk", None),
        P(None, ("blk", "grp"), None),
        P(None, "blk", None),
        P(None, ("blk", "grp")),
        P(None, ("blk", "grp")),
        P(None, ("blk", "grp"), None, None),
        P(None, ("blk", "grp"), None, None),
    )
    out_specs = (P(("blk", "grp"), None), P(("blk", "grp"), None))
    return jax.shard_map(functools.partial(body, mesh.shape["blk"]), mesh=mesh,
                         in_specs=in_specs, out_specs=out_specs, check_vma=False)
```

```python
import functools
import math

import jax
import jax.numpy as jnp
from jax import lax
from jax.experimental import pallas as pl
from jax.experimental.pallas import tpu as pltpu
from jax.sharding import PartitionSpec as P

STEP_SIZE = 0.001
LIKELIHOOD = 20.0
NOISE_SCALE = math.sqrt(0.002)
TILE = 128
FINE = 4
MESH = pl.DeviceIdType.MESH
F32 = jnp.float32
BF16 = jnp.bfloat16

(S0_SIB_FAR, S0_X, S0_SIB_OWN, FORWARD, RELAY_SIB, RELAY_X, RELAY_LAST,
 S1_SIB_FAR, S1_X, S1_SIB_OWN, FINAL) = range(11)
KINDS = 11
ON_CHIP = (S0_SIB_FAR, S0_SIB_OWN, RELAY_SIB, RELAY_LAST, S1_SIB_FAR, S1_SIB_OWN)


def halves(value):
    high = value.astype(BF16)
    low = (value - high.astype(F32)).astype(BF16)
    return high, low


def dot(left, right, contract):
    return lax.dot_general(left, right, (contract, ((), ())), preferred_element_type=F32)


def left_triple(value, axis):
    high, low = halves(value)
    return jnp.concatenate([high, low, high], axis=axis)


def right_triple(value, axis):
    high, low = halves(value)
    return jnp.concatenate([high, high, low], axis=axis)


def kernel(n_blk, tiles_hbm, counts_hbm, users_hbm, items_hbm, noise_users_hbm, noise_items_hbm,
           ratings_hbm, weights_hbm, users_out, items_out,
           tiles, counts, table, users, blocks, noise_users, noise_items, ratings0, weights0, ratings1, weights1,
           u_wide, u_tall, v_tall, e_wide, part, from_sib_far, from_x,
           from_sib_own, moved, local_sem, out_sem, send_sem, recv_sem):
    quarter = users.shape[0]
    per = quarter // TILE
    items = blocks.at[0]
    position = blocks.at[1]
    item_tiles = items.shape[0] // TILE
    slots = tiles.shape[1]
    blk = lax.axis_index("blk")
    grp = lax.axis_index("grp")
    side = grp // 2
    core = grp % 2
    sibling = (blk, side * 2 + (1 - core))
    across = (blk, (1 - side) * 2 + core)
    ahead = ((blk + 1) % n_blk, grp)
    behind = ((blk + n_blk - 1) % n_blk, grp)
    q_a = (1 - side) * 2 + core
    q_b = (1 - side) * 2 + (1 - core)
    q_c = side * 2 + core
    q_d = side * 2 + (1 - core)

    def rows(q, start=0, size=quarter):
        return pl.ds(pl.multiple_of(q * quarter + start, size), size)

    def chunk(kind):
        return TILE if kind in ON_CHIP else quarter // FINE

    def count(kind):
        return quarter // chunk(kind)

    def load(index, source, target):
        copy = pltpu.make_async_copy(source, target, local_sem.at[index])
        copy.start()
        return copy

    load_tiles = load(0, tiles_hbm, tiles)
    load_counts = load(1, counts_hbm, counts)
    load_users = load(2, users_hbm, users)
    load_items = [load(3, items_hbm.at[rows(q_d)], items.at[rows(q_d)])]
    load_ratings = [load(4, ratings_hbm.at[0], ratings0)]
    load_weights = [load(5, weights_hbm.at[0], weights0)]
    barrier = pltpu.get_barrier_semaphore()
    for other in (sibling, across, ahead, behind):
        pl.semaphore_signal(barrier, inc=1, device_id=other, device_id_type=MESH)
    for index, q in ((6, q_c), (7, q_b), (8, q_a)):
        load_items.append(load(index, items_hbm.at[rows(q)], items.at[rows(q)]))
    load_noise_users = load(9, noise_users_hbm, noise_users)
    load_noise_items = [load(10, noise_items_hbm.at[0, rows(q_a)], noise_items.at[0]),
                        load(11, noise_items_hbm.at[1, rows(q_c)], noise_items.at[1])]

    load_ratings.append(load(12, ratings_hbm.at[1], ratings1))
    load_weights.append(load(13, weights_hbm.at[1], weights1))

    def remote(kind, k, source, target, device):
        return pltpu.make_async_remote_copy(
            src_ref=source, dst_ref=target, send_sem=send_sem.at[kind, k],
            recv_sem=recv_sem.at[kind, k], device_id=device, device_id_type=MESH)

    def copy_of(kind, k):
        size = chunk(kind)
        piece = pl.ds(k * size, size)
        s = 0 if kind < S1_SIB_FAR else 1
        if kind in (S0_SIB_FAR, S1_SIB_FAR):
            return remote(kind, k, part.at[s, 0, piece], from_sib_far.at[s, piece], sibling)
        if kind in (S0_X, S1_X):
            return remote(kind, k, part.at[s, 1, piece], from_x.at[s, piece], across)
        if kind in (S0_SIB_OWN, S1_SIB_OWN):
            return remote(kind, k, part.at[s, 2, piece], from_sib_own.at[s, piece], sibling)
        if kind == FORWARD:
            return remote(kind, k, moved.at[0, piece], position.at[rows(q_a, k * size, size)], ahead)
        if kind == FINAL:
            return remote(kind, k, moved.at[1, piece], items_out.at[piece], ahead)
        where = rows(q_c if kind == RELAY_LAST else q_a, k * size, size)
        other = across if kind == RELAY_X else sibling
        return remote(kind, k, position.at[where], position.at[where], other)

    def send(kind, k):
        copy_of(kind, k).start()

    def arrive(kind, k):
        copy_of(kind, k).wait_recv()

    def fill_table(i, carry):
        stratum = i // (per * item_tiles)
        wanted = i % (per * item_tiles)
        slot = jnp.int32(-1)
        for s in range(slots):
            hit = jnp.logical_and(tiles[stratum, s] == wanted, s < counts[0, stratum])
            slot = jnp.where(hit, s, slot)
        table[i] = slot
        return carry

    def cell_err(stratum, row, column, predicted):
        slot = table[(stratum * per + row) * item_tiles + column]
        live = jnp.where(slot >= 0, jnp.float32(1), jnp.float32(0))
        slot = jnp.maximum(slot, 0)
        ratings, weights = ((ratings0, weights0), (ratings1, weights1))[stratum]
        return weights[slot].astype(F32) * live * (ratings[slot].astype(F32) - predicted)

    def grads(stratum, place, q, start, size):
        item_rows = blocks[stratum, rows(q, start, size), :]
        predicted = dot(u_wide[...], right_triple(item_rows, 1), ((1,), (1,)))
        bands = []
        for r in range(per):
            line = []
            for j in range(size // TILE):
                column = q * per + start // TILE + j
                line.append(cell_err(stratum, r, column,
                                     predicted[r * TILE:(r + 1) * TILE, j * TILE:(j + 1) * TILE]))
            bands.append(jnp.concatenate(line, axis=1))
        err = jnp.concatenate(bands, axis=0)
        part[stratum, place, pl.ds(start, size)] = dot(left_triple(err.T, 1), u_tall[...], ((1,), (0,)))
        item_high, item_low = halves(item_rows)
        err_high, err_low = halves(err)
        for third, item_part, err_part in ((0, item_high, err_high), (1, item_high, err_low),
                                           (2, item_low, err_high)):
            span = pl.ds(pl.multiple_of(third * quarter + start, size), size)
            v_tall[place, span] = item_part
            e_wide[place, :, span] = err_part

    def send_far(stratum, j):
        span = slice(j * TILE, (j + 1) * TILE)
        arrive((S0_SIB_FAR, S1_SIB_FAR)[stratum], j)
        part[stratum, 1, span] += from_sib_far[stratum, span]
        kind = (S0_X, S1_X)[stratum]
        for k in range(j * FINE // per, (j + 1) * FINE // per):
            send(kind, k)

    def split_users():
        now = users[...]
        u_wide[...] = left_triple(now, 1)
        u_tall[...] = right_triple(now, 0)

    def user_step(stratum):
        now = users[...]
        total = dot(jnp.concatenate([e_wide[p] for p in range(4)], axis=1),
                    jnp.concatenate([v_tall[p] for p in range(4)], axis=0), ((1,), (0,)))
        users[...] = now + STEP_SIZE * (LIKELIHOOD * total - now) + NOISE_SCALE * noise_users[stratum]

    def item_step(stratum, now, k):
        piece = pl.ds(k * quarter // FINE, quarter // FINE)
        arrive((S0_X, S1_X)[stratum], k)
        total = part[stratum, 3, piece] + from_sib_own[stratum, piece] + from_x[stratum, piece]
        moved[stratum, piece] = (now + STEP_SIZE * (LIKELIHOOD * total - now)
                                 + NOISE_SCALE * noise_items[stratum, piece])
        send((FORWARD, FINAL)[stratum], k)

    def relay(k):
        arrive(FORWARD, k)
        send(RELAY_X, k)
        if (k + 1) * per % FINE == 0:
            send(RELAY_SIB, (k + 1) * per // FINE - 1)

    def finish(stratum, q, k):
        fine = quarter // FINE
        if k * per % FINE == 0:
            arrive((S0_SIB_OWN, S1_SIB_OWN)[stratum], k * per // FINE)
        item_step(stratum, blocks[stratum, rows(q, k * fine, fine), :], k)

    def send_all(kind):
        for j in range(count(kind)):
            send(kind, j)

    def arrive_all(kind):
        for j in range(count(kind)):
            arrive(kind, j)

    load_tiles.wait()
    load_counts.wait()
    lax.fori_loop(0, 2 * per * item_tiles, fill_table, 0)
    load_users.wait()
    split_users()
    load_ratings[0].wait()
    load_weights[0].wait()
    pl.semaphore_wait(barrier, 4)

    def first(i, carry):
        for p in range(4):
            @pl.when(i == p)
            def _():
                load_items[p].wait()

        grads(0, i, jnp.where(i == 0, q_d, jnp.where(i == 1, q_c, jnp.where(i == 2, q_b, q_a))), 0, quarter)

        @pl.when(i == 0)
        def _():
            send_all(S0_SIB_FAR)

        @pl.when(i == 1)
        def _():
            for j in range(per):
                send_far(0, j)

        @pl.when(i == 2)
        def _():
            send_all(S0_SIB_OWN)

        return carry

    lax.fori_loop(0, 4, first, 0)
    load_noise_items[0].wait()
    finish(0, q_a, 0)
    load_noise_users.wait()
    user_step(0)
    split_users()
    for k in range(1, FINE):
        finish(0, q_a, k)
        if k >= 2:
            relay(k - 2)

    for k in range(FINE - 2, FINE):
        relay(k)
    load_ratings[1].wait()
    load_weights[1].wait()
    load_noise_items[1].wait()

    def second(i, carry):
        @pl.when(i == 0)
        def _():
            arrive_all(RELAY_SIB)

        @pl.when(i == 2)
        def _():
            for n in range(per):
                for k in range(n * FINE // per, (n + 1) * FINE // per):
                    arrive(RELAY_X, k)
                send(RELAY_LAST, n)

        @pl.when(i == 3)
        def _():
            arrive_all(RELAY_LAST)

        place = jnp.where(i < 2, i, 5 - i)
        q = jnp.where(i == 0, q_b, jnp.where(i == 1, q_a, jnp.where(i == 2, q_c, q_d)))
        grads(1, place, q, 0, quarter)

        @pl.when(i == 0)
        def _():
            send_all(S1_SIB_FAR)

        @pl.when(i == 1)
        def _():
            for n in range(per):
                send_far(1, n)

        @pl.when(i == 3)
        def _():
            send_all(S1_SIB_OWN)

        return carry

    lax.fori_loop(0, 4, second, 0)
    for k in range(FINE):
        finish(1, q_c, k)
    user_step(1)
    store = pltpu.make_async_copy(users, users_out, out_sem)
    store.start()
    for kind in range(KINDS):
        for k in range(count(kind)):
            copy_of(kind, k).wait_send()
    store.wait()
    arrive_all(FINAL)


def body(n_blk, users, items, noise_users, noise_items, tile_index, counts, ratings, weights):
    mine, rank = users.shape
    slots, tile = ratings.shape[1], ratings.shape[2]
    kept = (mine, rank)
    any_spec = pl.BlockSpec(memory_space=pl.ANY)
    work = 2 * 3 * 3 * 2 * mine * items.shape[0] * rank
    return pl.pallas_call(
        functools.partial(kernel, n_blk),
        out_shape=(pltpu.VMEM(kept, F32), pltpu.VMEM(kept, F32)),
        in_specs=[any_spec] * 8,
        out_specs=(any_spec, any_spec),
        scratch_shapes=[
            pltpu.SMEM(tile_index.shape, jnp.int32),
            pltpu.SMEM((1, counts.shape[0]), jnp.int32),
            pltpu.SMEM((2 * (mine // tile) * (items.shape[0] // tile),), jnp.int32),
            pltpu.VMEM(kept, F32),
            pltpu.VMEM((2,) + items.shape, F32),
            pltpu.VMEM((2,) + kept, F32),
            pltpu.VMEM((2,) + kept, F32),
            pltpu.VMEM((slots, tile, tile), BF16),
            pltpu.VMEM((slots, tile, tile), BF16),
            pltpu.VMEM((slots, tile, tile), BF16),
            pltpu.VMEM((slots, tile, tile), BF16),
            pltpu.VMEM((mine, 3 * rank), BF16),
            pltpu.VMEM((3 * mine, rank), BF16),
            pltpu.VMEM((4, 3 * mine, rank), BF16),
            pltpu.VMEM((4, mine, 3 * mine), BF16),
            pltpu.VMEM((2, 4) + kept, F32),
            pltpu.VMEM((2,) + kept, F32),
            pltpu.VMEM((2,) + kept, F32),
            pltpu.VMEM((2,) + kept, F32),
            pltpu.VMEM((2,) + kept, F32),
            pltpu.SemaphoreType.DMA((14,)),
            pltpu.SemaphoreType.DMA,
            pltpu.SemaphoreType.DMA((KINDS, FINE)),
            pltpu.SemaphoreType.DMA((KINDS, FINE)),
        ],
        compiler_params=pltpu.CompilerParams(
            collective_id=0, has_side_effects=True, vmem_limit_bytes=56 * 1024 * 1024),
        cost_estimate=pl.CostEstimate(flops=work, bytes_accessed=4 * 2 ** 20, transcendentals=0),
    )(tile_index, counts.T, users, items, noise_users, noise_items, ratings, weights)


def solution(mesh):
    in_specs = (
        P(("blk", "grp"), None),
        P("blk", None),
        P(None, ("blk", "grp"), None),
        P(None, "blk", None),
        P(None, ("blk", "grp")),
        P(None, ("blk", "grp")),
        P(None, ("blk", "grp"), None, None),
        P(None, ("blk", "grp"), None, None),
    )
    out_specs = (P(("blk", "grp"), None), P(("blk", "grp"), None))
    return jax.shard_map(functools.partial(body, mesh.shape["blk"]), mesh=mesh,
                         in_specs=in_specs, out_specs=out_specs, check_vma=False)
```

```python
import functools
import math

import jax
import jax.numpy as jnp
from jax import lax
from jax.experimental import pallas as pl
from jax.experimental.pallas import tpu as pltpu
from jax.sharding import PartitionSpec as P

STEP_SIZE = 0.001
LIKELIHOOD = 20.0
NOISE_SCALE = math.sqrt(0.002)
TILE = 128
FINE = 4
MESH = pl.DeviceIdType.MESH
F32 = jnp.float32
BF16 = jnp.bfloat16

(S0_SIB_FAR, S0_X, S0_SIB_OWN, FORWARD, RELAY_SIB, RELAY_X, RELAY_LAST,
 S1_SIB_FAR, S1_X, S1_SIB_OWN, FINAL) = range(11)
KINDS = 11
ON_CHIP = (S0_SIB_FAR, S0_SIB_OWN, RELAY_SIB, RELAY_LAST, S1_SIB_FAR, S1_SIB_OWN)


def halves(value):
    high = value.astype(BF16)
    low = (value - high.astype(F32)).astype(BF16)
    return high, low


def dot(left, right, contract):
    return lax.dot_general(left, right, (contract, ((), ())), preferred_element_type=F32)


def left_triple(value, axis):
    high, low = halves(value)
    return jnp.concatenate([high, low, high], axis=axis)


def right_triple(value, axis):
    high, low = halves(value)
    return jnp.concatenate([high, high, low], axis=axis)


def kernel(n_blk, tiles_hbm, counts_hbm, users_hbm, items_hbm, noise_users_hbm, noise_items_hbm,
           ratings_hbm, weights_hbm, users_out, items_out,
           tiles, counts, table, users, blocks, noise_users, noise_items, ratings0, weights0, ratings1, weights1,
           u_wide, u_tall, v_tall, e_wide, part, from_sib_far, from_x,
           from_sib_own, moved, local_sem, out_sem, send_sem, recv_sem):
    quarter = users.shape[0]
    per = quarter // TILE
    items = blocks.at[0]
    position = blocks.at[1]
    item_tiles = items.shape[0] // TILE
    slots = tiles.shape[1]
    blk = lax.axis_index("blk")
    grp = lax.axis_index("grp")
    side = grp // 2
    core = grp % 2
    sibling = (blk, side * 2 + (1 - core))
    across = (blk, (1 - side) * 2 + core)
    ahead = ((blk + 1) % n_blk, grp)
    behind = ((blk + n_blk - 1) % n_blk, grp)
    q_a = (1 - side) * 2 + core
    q_b = (1 - side) * 2 + (1 - core)
    q_c = side * 2 + core
    q_d = side * 2 + (1 - core)

    def rows(q, start=0, size=quarter):
        return pl.ds(pl.multiple_of(q * quarter + start, size), size)

    def chunk(kind):
        return TILE if kind in ON_CHIP else quarter // FINE

    def count(kind):
        return quarter // chunk(kind)

    def load(index, source, target):
        copy = pltpu.make_async_copy(source, target, local_sem.at[index])
        copy.start()
        return copy

    load_tiles = load(0, tiles_hbm, tiles)
    load_counts = load(1, counts_hbm, counts)
    load_users = load(2, users_hbm, users)
    load_items = [load(3, items_hbm.at[rows(q_d)], items.at[rows(q_d)])]
    load_ratings = [load(4, ratings_hbm.at[0], ratings0)]
    load_weights = [load(5, weights_hbm.at[0], weights0)]
    barrier = pltpu.get_barrier_semaphore()
    for other in (sibling, across, ahead, behind):
        pl.semaphore_signal(barrier, inc=1, device_id=other, device_id_type=MESH)
    for index, q in ((6, q_c), (7, q_b), (8, q_a)):
        load_items.append(load(index, items_hbm.at[rows(q)], items.at[rows(q)]))
    load_noise_users = load(9, noise_users_hbm, noise_users)
    load_noise_items = [load(10, noise_items_hbm.at[0, rows(q_a)], noise_items.at[0]),
                        load(11, noise_items_hbm.at[1, rows(q_c)], noise_items.at[1])]

    load_ratings.append(load(12, ratings_hbm.at[1], ratings1))
    load_weights.append(load(13, weights_hbm.at[1], weights1))

    def remote(kind, k, source, target, device):
        return pltpu.make_async_remote_copy(
            src_ref=source, dst_ref=target, send_sem=send_sem.at[kind, k],
            recv_sem=recv_sem.at[kind, k], device_id=device, device_id_type=MESH)

    def copy_of(kind, k):
        size = chunk(kind)
        piece = pl.ds(k * size, size)
        s = 0 if kind < S1_SIB_FAR else 1
        if kind in (S0_SIB_FAR, S1_SIB_FAR):
            return remote(kind, k, part.at[s, 0, piece], from_sib_far.at[s, piece], sibling)
        if kind in (S0_X, S1_X):
            return remote(kind, k, part.at[s, 1, piece], from_x.at[s, piece], across)
        if kind in (S0_SIB_OWN, S1_SIB_OWN):
            return remote(kind, k, part.at[s, 2, piece], from_sib_own.at[s, piece], sibling)
        if kind == FORWARD:
            return remote(kind, k, moved.at[0, piece], position.at[rows(q_a, k * size, size)], ahead)
        if kind == FINAL:
            return remote(kind, k, moved.at[1, piece], items_out.at[piece], ahead)
        where = rows(q_c if kind == RELAY_LAST else q_a, k * size, size)
        other = across if kind == RELAY_X else sibling
        return remote(kind, k, position.at[where], position.at[where], other)

    def send(kind, k):
        copy_of(kind, k).start()

    def arrive(kind, k):
        copy_of(kind, k).wait_recv()

    def fill_table(i, carry):
        stratum = i // (per * item_tiles)
        wanted = i % (per * item_tiles)
        slot = jnp.int32(-1)
        for s in range(slots):
            hit = jnp.logical_and(tiles[stratum, s] == wanted, s < counts[0, stratum])
            slot = jnp.where(hit, s, slot)
        table[i] = slot
        return carry

    def cell_err(stratum, row, column, predicted):
        slot = table[(stratum * per + row) * item_tiles + column]
        live = jnp.where(slot >= 0, jnp.float32(1), jnp.float32(0))
        slot = jnp.maximum(slot, 0)
        ratings, weights = ((ratings0, weights0), (ratings1, weights1))[stratum]
        return weights[slot].astype(F32) * live * (ratings[slot].astype(F32) - predicted)

    def grads(stratum, place, q, start, size):
        item_rows = blocks[stratum, rows(q, start, size), :]
        predicted = dot(u_wide[...], right_triple(item_rows, 1), ((1,), (1,)))
        bands = []
        for r in range(per):
            line = []
            for j in range(size // TILE):
                column = q * per + start // TILE + j
                line.append(cell_err(stratum, r, column,
                                     predicted[r * TILE:(r + 1) * TILE, j * TILE:(j + 1) * TILE]))
            bands.append(jnp.concatenate(line, axis=1))
        err = jnp.concatenate(bands, axis=0)
        part[stratum, place, pl.ds(start, size)] = dot(left_triple(err.T, 1), u_tall[...], ((1,), (0,)))
        item_high, item_low = halves(item_rows)
        err_high, err_low = halves(err)
        for third, item_part, err_part in ((0, item_high, err_high), (1, item_high, err_low),
                                           (2, item_low, err_high)):
            span = pl.ds(pl.multiple_of(third * quarter + start, size), size)
            v_tall[place, span] = item_part
            e_wide[place, :, span] = err_part

    def send_far(stratum, j):
        span = slice(j * TILE, (j + 1) * TILE)
        arrive((S0_SIB_FAR, S1_SIB_FAR)[stratum], j)
        part[stratum, 1, span] += from_sib_far[stratum, span]
        kind = (S0_X, S1_X)[stratum]
        for k in range(j * FINE // per, (j + 1) * FINE // per):
            send(kind, k)

    def split_users():
        now = users[...]
        u_wide[...] = left_triple(now, 1)
        u_tall[...] = right_triple(now, 0)

    def user_step(stratum):
        now = users[...]
        total = dot(jnp.concatenate([e_wide[p] for p in range(4)], axis=1),
                    jnp.concatenate([v_tall[p] for p in range(4)], axis=0), ((1,), (0,)))
        users[...] = now + STEP_SIZE * (LIKELIHOOD * total - now) + NOISE_SCALE * noise_users[stratum]

    def item_step(stratum, now, k):
        piece = pl.ds(k * quarter // FINE, quarter // FINE)
        arrive((S0_X, S1_X)[stratum], k)
        total = part[stratum, 3, piece] + from_sib_own[stratum, piece] + from_x[stratum, piece]
        moved[stratum, piece] = (now + STEP_SIZE * (LIKELIHOOD * total - now)
                                 + NOISE_SCALE * noise_items[stratum, piece])
        send((FORWARD, FINAL)[stratum], k)

    def relay(k):
        arrive(FORWARD, k)
        if (k + 1) * per % FINE == 0:
            send(RELAY_SIB, (k + 1) * per // FINE - 1)
        send(RELAY_X, k)

    def finish(stratum, q, k):
        fine = quarter // FINE
        if k * per % FINE == 0:
            arrive((S0_SIB_OWN, S1_SIB_OWN)[stratum], k * per // FINE)
        item_step(stratum, blocks[stratum, rows(q, k * fine, fine), :], k)

    def send_all(kind):
        for j in range(count(kind)):
            send(kind, j)

    def arrive_all(kind):
        for j in range(count(kind)):
            arrive(kind, j)

    load_tiles.wait()
    load_counts.wait()
    lax.fori_loop(0, 2 * per * item_tiles, fill_table, 0)
    load_users.wait()
    split_users()
    load_ratings[0].wait()
    load_weights[0].wait()
    pl.semaphore_wait(barrier, 4)

    def first(i, carry):
        for p in range(4):
            @pl.when(i == p)
            def _():
                load_items[(0, 2, 1, 3)[p]].wait()

        place = jnp.where(i == 1, 2, jnp.where(i == 2, 1, i))
        q = jnp.where(i == 0, q_d, jnp.where(i == 1, q_b, jnp.where(i == 2, q_c, q_a)))
        grads(0, place, q, 0, quarter)

        @pl.when(i == 0)
        def _():
            send_all(S0_SIB_FAR)

        @pl.when(i == 1)
        def _():
            send_all(S0_SIB_OWN)

        @pl.when(i == 2)
        def _():
            for j in range(per):
                send_far(0, j)

        return carry

    lax.fori_loop(0, 4, first, 0)
    load_noise_items[0].wait()
    finish(0, q_a, 0)
    load_noise_users.wait()
    user_step(0)
    split_users()
    for k in range(1, FINE):
        finish(0, q_a, k)
        if k >= 2:
            relay(k - 2)

    for k in range(FINE - 2, FINE):
        relay(k)
    load_ratings[1].wait()
    load_weights[1].wait()
    load_noise_items[1].wait()

    def second(i, carry):
        @pl.when(i == 0)
        def _():
            arrive_all(RELAY_SIB)

        @pl.when(i == 2)
        def _():
            for n in range(per):
                for k in range(n * FINE // per, (n + 1) * FINE // per):
                    arrive(RELAY_X, k)
                send(RELAY_LAST, n)

        @pl.when(i == 3)
        def _():
            arrive_all(RELAY_LAST)

        place = jnp.where(i < 2, i, 5 - i)
        q = jnp.where(i == 0, q_b, jnp.where(i == 1, q_a, jnp.where(i == 2, q_c, q_d)))
        grads(1, place, q, 0, quarter)

        @pl.when(i == 0)
        def _():
            send_all(S1_SIB_FAR)

        @pl.when(i == 1)
        def _():
            for n in range(per):
                send_far(1, n)

        @pl.when(i == 3)
        def _():
            send_all(S1_SIB_OWN)

        return carry

    lax.fori_loop(0, 4, second, 0)
    for k in range(FINE):
        finish(1, q_c, k)
    user_step(1)
    store = pltpu.make_async_copy(users, users_out, out_sem)
    store.start()
    for kind in range(KINDS):
        for k in range(count(kind)):
            copy_of(kind, k).wait_send()
    store.wait()
    arrive_all(FINAL)


def body(n_blk, users, items, noise_users, noise_items, tile_index, counts, ratings, weights):
    mine, rank = users.shape
    slots, tile = ratings.shape[1], ratings.shape[2]
    kept = (mine, rank)
    any_spec = pl.BlockSpec(memory_space=pl.ANY)
    work = 2 * 3 * 3 * 2 * mine * items.shape[0] * rank
    return pl.pallas_call(
        functools.partial(kernel, n_blk),
        out_shape=(pltpu.VMEM(kept, F32), pltpu.VMEM(kept, F32)),
        in_specs=[any_spec] * 8,
        out_specs=(any_spec, any_spec),
        scratch_shapes=[
            pltpu.SMEM(tile_index.shape, jnp.int32),
            pltpu.SMEM((1, counts.shape[0]), jnp.int32),
            pltpu.SMEM((2 * (mine // tile) * (items.shape[0] // tile),), jnp.int32),
            pltpu.VMEM(kept, F32),
            pltpu.VMEM((2,) + items.shape, F32),
            pltpu.VMEM((2,) + kept, F32),
            pltpu.VMEM((2,) + kept, F32),
            pltpu.VMEM((slots, tile, tile), BF16),
            pltpu.VMEM((slots, tile, tile), BF16),
            pltpu.VMEM((slots, tile, tile), BF16),
            pltpu.VMEM((slots, tile, tile), BF16),
            pltpu.VMEM((mine, 3 * rank), BF16),
            pltpu.VMEM((3 * mine, rank), BF16),
            pltpu.VMEM((4, 3 * mine, rank), BF16),
            pltpu.VMEM((4, mine, 3 * mine), BF16),
            pltpu.VMEM((2, 4) + kept, F32),
            pltpu.VMEM((2,) + kept, F32),
            pltpu.VMEM((2,) + kept, F32),
            pltpu.VMEM((2,) + kept, F32),
            pltpu.VMEM((2,) + kept, F32),
            pltpu.SemaphoreType.DMA((14,)),
            pltpu.SemaphoreType.DMA,
            pltpu.SemaphoreType.DMA((KINDS, FINE)),
            pltpu.SemaphoreType.DMA((KINDS, FINE)),
        ],
        compiler_params=pltpu.CompilerParams(
            collective_id=0, has_side_effects=True, vmem_limit_bytes=56 * 1024 * 1024),
        cost_estimate=pl.CostEstimate(flops=work, bytes_accessed=4 * 2 ** 20, transcendentals=0),
    )(tile_index, counts.T, users, items, noise_users, noise_items, ratings, weights)


def solution(mesh):
    in_specs = (
        P(("blk", "grp"), None),
        P("blk", None),
        P(None, ("blk", "grp"), None),
        P(None, "blk", None),
        P(None, ("blk", "grp")),
        P(None, ("blk", "grp")),
        P(None, ("blk", "grp"), None, None),
        P(None, ("blk", "grp"), None, None),
    )
    out_specs = (P(("blk", "grp"), None), P(("blk", "grp"), None))
    return jax.shard_map(functools.partial(body, mesh.shape["blk"]), mesh=mesh,
                         in_specs=in_specs, out_specs=out_specs, check_vma=False)
```

```python
import functools
import math

import jax
import jax.numpy as jnp
from jax import lax
from jax.experimental import pallas as pl
from jax.experimental.pallas import tpu as pltpu
from jax.sharding import PartitionSpec as P

STEP_SIZE = 0.001
LIKELIHOOD = 20.0
NOISE_SCALE = math.sqrt(0.002)
TILE = 128
FINE = 8
LAG = FINE // 2
MESH = pl.DeviceIdType.MESH
F32 = jnp.float32
BF16 = jnp.bfloat16

(S0_SIB_FAR, S0_X, S0_SIB_OWN, FORWARD, RELAY_SIB, RELAY_X, RELAY_LAST,
 S1_SIB_FAR, S1_X, S1_SIB_OWN, FINAL) = range(11)
KINDS = 11
ON_CHIP = (S0_SIB_FAR, S0_SIB_OWN, RELAY_SIB, RELAY_LAST, S1_SIB_FAR, S1_SIB_OWN)


def halves(value):
    high = value.astype(BF16)
    low = (value - high.astype(F32)).astype(BF16)
    return high, low


def dot(left, right, contract):
    return lax.dot_general(left, right, (contract, ((), ())), preferred_element_type=F32)


def left_triple(value, axis):
    high, low = halves(value)
    return jnp.concatenate([high, low, high], axis=axis)


def right_triple(value, axis):
    high, low = halves(value)
    return jnp.concatenate([high, high, low], axis=axis)


def kernel(n_blk, tiles_hbm, counts_hbm, users_hbm, items_hbm, noise_users_hbm, noise_items_hbm,
           ratings_hbm, weights_hbm, users_out, items_out,
           tiles, counts, table, users, blocks, noise_users, noise_items, ratings0, weights0, ratings1, weights1,
           u_wide, u_tall, v_tall, e_wide, part, from_sib_far, from_x,
           from_sib_own, moved, local_sem, out_sem, send_sem, recv_sem):
    quarter = users.shape[0]
    per = quarter // TILE
    items = blocks.at[0]
    position = blocks.at[1]
    item_tiles = items.shape[0] // TILE
    slots = tiles.shape[1]
    blk = lax.axis_index("blk")
    grp = lax.axis_index("grp")
    side = grp // 2
    core = grp % 2
    sibling = (blk, side * 2 + (1 - core))
    across = (blk, (1 - side) * 2 + core)
    ahead = ((blk + 1) % n_blk, grp)
    behind = ((blk + n_blk - 1) % n_blk, grp)
    q_a = (1 - side) * 2 + core
    q_b = (1 - side) * 2 + (1 - core)
    q_c = side * 2 + core
    q_d = side * 2 + (1 - core)

    def rows(q, start=0, size=quarter):
        return pl.ds(pl.multiple_of(q * quarter + start, size), size)

    def chunk(kind):
        return TILE if kind in ON_CHIP else quarter // FINE

    def count(kind):
        return quarter // chunk(kind)

    def load(index, source, target):
        copy = pltpu.make_async_copy(source, target, local_sem.at[index])
        copy.start()
        return copy

    load_tiles = load(0, tiles_hbm, tiles)
    load_counts = load(1, counts_hbm, counts)
    load_users = load(2, users_hbm, users)
    load_items = [load(3, items_hbm.at[rows(q_d)], items.at[rows(q_d)])]
    load_ratings = [load(4, ratings_hbm.at[0], ratings0)]
    load_weights = [load(5, weights_hbm.at[0], weights0)]
    barrier = pltpu.get_barrier_semaphore()
    for other in (sibling, across, ahead, behind):
        pl.semaphore_signal(barrier, inc=1, device_id=other, device_id_type=MESH)
    for index, q in ((6, q_c), (7, q_b), (8, q_a)):
        load_items.append(load(index, items_hbm.at[rows(q)], items.at[rows(q)]))
    load_noise_users = load(9, noise_users_hbm, noise_users)
    load_noise_items = [load(10, noise_items_hbm.at[0, rows(q_a)], noise_items.at[0]),
                        load(11, noise_items_hbm.at[1, rows(q_c)], noise_items.at[1])]

    load_ratings.append(load(12, ratings_hbm.at[1], ratings1))
    load_weights.append(load(13, weights_hbm.at[1], weights1))

    def remote(kind, k, source, target, device):
        return pltpu.make_async_remote_copy(
            src_ref=source, dst_ref=target, send_sem=send_sem.at[kind, k],
            recv_sem=recv_sem.at[kind, k], device_id=device, device_id_type=MESH)

    def copy_of(kind, k):
        size = chunk(kind)
        piece = pl.ds(k * size, size)
        s = 0 if kind < S1_SIB_FAR else 1
        if kind in (S0_SIB_FAR, S1_SIB_FAR):
            return remote(kind, k, part.at[s, 0, piece], from_sib_far.at[s, piece], sibling)
        if kind in (S0_X, S1_X):
            return remote(kind, k, part.at[s, 1, piece], from_x.at[s, piece], across)
        if kind in (S0_SIB_OWN, S1_SIB_OWN):
            return remote(kind, k, part.at[s, 2, piece], from_sib_own.at[s, piece], sibling)
        if kind == FORWARD:
            return remote(kind, k, moved.at[0, piece], position.at[rows(q_a, k * size, size)], ahead)
        if kind == FINAL:
            return remote(kind, k, moved.at[1, piece], items_out.at[piece], ahead)
        where = rows(q_c if kind == RELAY_LAST else q_a, k * size, size)
        other = across if kind == RELAY_X else sibling
        return remote(kind, k, position.at[where], position.at[where], other)

    def send(kind, k):
        copy_of(kind, k).start()

    def arrive(kind, k):
        copy_of(kind, k).wait_recv()

    def fill_table(i, carry):
        stratum = i // (per * item_tiles)
        wanted = i % (per * item_tiles)
        slot = jnp.int32(-1)
        for s in range(slots):
            hit = jnp.logical_and(tiles[stratum, s] == wanted, s < counts[0, stratum])
            slot = jnp.where(hit, s, slot)
        table[i] = slot
        return carry

    def cell_err(stratum, row, column, predicted):
        slot = table[(stratum * per + row) * item_tiles + column]
        live = jnp.where(slot >= 0, jnp.float32(1), jnp.float32(0))
        slot = jnp.maximum(slot, 0)
        ratings, weights = ((ratings0, weights0), (ratings1, weights1))[stratum]
        return weights[slot].astype(F32) * live * (ratings[slot].astype(F32) - predicted)

    def grads(stratum, place, q, start, size):
        item_rows = blocks[stratum, rows(q, start, size), :]
        predicted = dot(u_wide[...], right_triple(item_rows, 1), ((1,), (1,)))
        bands = []
        for r in range(per):
            line = []
            for j in range(size // TILE):
                column = q * per + start // TILE + j
                line.append(cell_err(stratum, r, column,
                                     predicted[r * TILE:(r + 1) * TILE, j * TILE:(j + 1) * TILE]))
            bands.append(jnp.concatenate(line, axis=1))
        err = jnp.concatenate(bands, axis=0)
        part[stratum, place, pl.ds(start, size)] = dot(left_triple(err.T, 1), u_tall[...], ((1,), (0,)))
        item_high, item_low = halves(item_rows)
        err_high, err_low = halves(err)
        for third, item_part, err_part in ((0, item_high, err_high), (1, item_high, err_low),
                                           (2, item_low, err_high)):
            span = pl.ds(pl.multiple_of(third * quarter + start, size), size)
            v_tall[place, span] = item_part
            e_wide[place, :, span] = err_part

    def send_far(stratum, j):
        span = slice(j * TILE, (j + 1) * TILE)
        arrive((S0_SIB_FAR, S1_SIB_FAR)[stratum], j)
        part[stratum, 1, span] += from_sib_far[stratum, span]
        kind = (S0_X, S1_X)[stratum]
        for k in range(j * FINE // per, (j + 1) * FINE // per):
            send(kind, k)

    def split_users():
        now = users[...]
        u_wide[...] = left_triple(now, 1)
        u_tall[...] = right_triple(now, 0)

    def user_step(stratum):
        now = users[...]
        total = dot(jnp.concatenate([e_wide[p] for p in range(4)], axis=1),
                    jnp.concatenate([v_tall[p] for p in range(4)], axis=0), ((1,), (0,)))
        users[...] = now + STEP_SIZE * (LIKELIHOOD * total - now) + NOISE_SCALE * noise_users[stratum]

    def item_step(stratum, now, k):
        piece = pl.ds(k * quarter // FINE, quarter // FINE)
        arrive((S0_X, S1_X)[stratum], k)
        total = part[stratum, 3, piece] + from_sib_own[stratum, piece] + from_x[stratum, piece]
        moved[stratum, piece] = (now + STEP_SIZE * (LIKELIHOOD * total - now)
                                 + NOISE_SCALE * noise_items[stratum, piece])
        send((FORWARD, FINAL)[stratum], k)

    def relay(k):
        arrive(FORWARD, k)
        send(RELAY_X, k)
        if (k + 1) * per % FINE == 0:
            send(RELAY_SIB, (k + 1) * per // FINE - 1)

    def finish(stratum, q, k):
        fine = quarter // FINE
        if k * per % FINE == 0:
            arrive((S0_SIB_OWN, S1_SIB_OWN)[stratum], k * per // FINE)
        item_step(stratum, blocks[stratum, rows(q, k * fine, fine), :], k)

    def send_all(kind):
        for j in range(count(kind)):
            send(kind, j)

    def arrive_all(kind):
        for j in range(count(kind)):
            arrive(kind, j)

    load_tiles.wait()
    load_counts.wait()
    lax.fori_loop(0, 2 * per * item_tiles, fill_table, 0)
    load_users.wait()
    split_users()
    load_ratings[0].wait()
    load_weights[0].wait()
    pl.semaphore_wait(barrier, 4)

    def first(i, carry):
        for p in range(4):
            @pl.when(i == p)
            def _():
                load_items[p].wait()

        grads(0, i, jnp.where(i == 0, q_d, jnp.where(i == 1, q_c, jnp.where(i == 2, q_b, q_a))), 0, quarter)

        @pl.when(i == 0)
        def _():
            send_all(S0_SIB_FAR)

        @pl.when(i == 1)
        def _():
            for j in range(per):
                send_far(0, j)

        @pl.when(i == 2)
        def _():
            send_all(S0_SIB_OWN)

        return carry

    lax.fori_loop(0, 4, first, 0)
    load_noise_items[0].wait()
    finish(0, q_a, 0)
    load_noise_users.wait()
    user_step(0)
    split_users()
    for k in range(1, FINE):
        finish(0, q_a, k)
        if k >= LAG:
            relay(k - LAG)

    for k in range(FINE - LAG, FINE):
        relay(k)
    load_ratings[1].wait()
    load_weights[1].wait()
    load_noise_items[1].wait()

    def second(i, carry):
        @pl.when(i == 0)
        def _():
            arrive_all(RELAY_SIB)

        @pl.when(i == 2)
        def _():
            for n in range(per):
                for k in range(n * FINE // per, (n + 1) * FINE // per):
                    arrive(RELAY_X, k)
                send(RELAY_LAST, n)

        @pl.when(i == 3)
        def _():
            arrive_all(RELAY_LAST)

        place = jnp.where(i < 2, i, 5 - i)
        q = jnp.where(i == 0, q_b, jnp.where(i == 1, q_a, jnp.where(i == 2, q_c, q_d)))
        grads(1, place, q, 0, quarter)

        @pl.when(i == 0)
        def _():
            send_all(S1_SIB_FAR)

        @pl.when(i == 1)
        def _():
            for n in range(per):
                send_far(1, n)

        @pl.when(i == 3)
        def _():
            send_all(S1_SIB_OWN)

        return carry

    lax.fori_loop(0, 4, second, 0)
    for k in range(FINE):
        finish(1, q_c, k)
    user_step(1)
    store = pltpu.make_async_copy(users, users_out, out_sem)
    store.start()
    for kind in range(KINDS):
        for k in range(count(kind)):
            copy_of(kind, k).wait_send()
    store.wait()
    arrive_all(FINAL)


def body(n_blk, users, items, noise_users, noise_items, tile_index, counts, ratings, weights):
    mine, rank = users.shape
    slots, tile = ratings.shape[1], ratings.shape[2]
    kept = (mine, rank)
    any_spec = pl.BlockSpec(memory_space=pl.ANY)
    work = 2 * 3 * 3 * 2 * mine * items.shape[0] * rank
    return pl.pallas_call(
        functools.partial(kernel, n_blk),
        out_shape=(pltpu.VMEM(kept, F32), pltpu.VMEM(kept, F32)),
        in_specs=[any_spec] * 8,
        out_specs=(any_spec, any_spec),
        scratch_shapes=[
            pltpu.SMEM(tile_index.shape, jnp.int32),
            pltpu.SMEM((1, counts.shape[0]), jnp.int32),
            pltpu.SMEM((2 * (mine // tile) * (items.shape[0] // tile),), jnp.int32),
            pltpu.VMEM(kept, F32),
            pltpu.VMEM((2,) + items.shape, F32),
            pltpu.VMEM((2,) + kept, F32),
            pltpu.VMEM((2,) + kept, F32),
            pltpu.VMEM((slots, tile, tile), BF16),
            pltpu.VMEM((slots, tile, tile), BF16),
            pltpu.VMEM((slots, tile, tile), BF16),
            pltpu.VMEM((slots, tile, tile), BF16),
            pltpu.VMEM((mine, 3 * rank), BF16),
            pltpu.VMEM((3 * mine, rank), BF16),
            pltpu.VMEM((4, 3 * mine, rank), BF16),
            pltpu.VMEM((4, mine, 3 * mine), BF16),
            pltpu.VMEM((2, 4) + kept, F32),
            pltpu.VMEM((2,) + kept, F32),
            pltpu.VMEM((2,) + kept, F32),
            pltpu.VMEM((2,) + kept, F32),
            pltpu.VMEM((2,) + kept, F32),
            pltpu.SemaphoreType.DMA((14,)),
            pltpu.SemaphoreType.DMA,
            pltpu.SemaphoreType.DMA((KINDS, FINE)),
            pltpu.SemaphoreType.DMA((KINDS, FINE)),
        ],
        compiler_params=pltpu.CompilerParams(
            collective_id=0, has_side_effects=True, vmem_limit_bytes=56 * 1024 * 1024),
        cost_estimate=pl.CostEstimate(flops=work, bytes_accessed=4 * 2 ** 20, transcendentals=0),
    )(tile_index, counts.T, users, items, noise_users, noise_items, ratings, weights)


def solution(mesh):
    in_specs = (
        P(("blk", "grp"), None),
        P("blk", None),
        P(None, ("blk", "grp"), None),
        P(None, "blk", None),
        P(None, ("blk", "grp")),
        P(None, ("blk", "grp")),
        P(None, ("blk", "grp"), None, None),
        P(None, ("blk", "grp"), None, None),
    )
    out_specs = (P(("blk", "grp"), None), P(("blk", "grp"), None))
    return jax.shard_map(functools.partial(body, mesh.shape["blk"]), mesh=mesh,
                         in_specs=in_specs, out_specs=out_specs, check_vma=False)
```
